256 devices in a mesh: dp: 32 (over y, z), grp: 8 (over x, core).
Axes of the slice: x: 4, y: 4, z: 8, core: 2. Of those that a mesh axis runs over, the one named last changes fastest.
Arguments:
- query_in: bfloat16 [32768, 2048], P(('dp', 'grp')), may hold values from -6 to 6
- key_in: bfloat16 [32768, 2048], P(('dp', 'grp')), may hold values from -6 to 6
- value_in: bfloat16 [32768, 2048], P(('dp', 'grp')), may hold values from -6 to 6
- out_grad: bfloat16 [32768, 2048], P(('dp', 'grp')), may hold values from -6 to 6
- query_gain: float32 [128], replicated, may hold values from 1.5 to 2.5
- key_gain: float32 [128], replicated, may hold values from 1.5 to 2.5
- positions: int32 [3, 32768], P(None, ('dp', 'grp')), may hold values from 0 to 63
- token_place: int32 [32768], P(('dp', 'grp')), may hold values from 0 to 32767, as said below
- clip_index: int32 [32, 1024], P('dp'), may hold values from 0 to 1, never falling along the last dimension, each value on 1 to 768 neighbouring positions
Outputs:
- attention: bfloat16 [32768, 2048], P(('dp', 'grp'))
- grad_query: bfloat16 [32768, 2048], P(('dp', 'grp'))
- grad_key: bfloat16 [32768, 2048], P(('dp', 'grp'))
- grad_value: bfloat16 [32768, 2048], P(('dp', 'grp'))
The draws below stay inside these ranges and needn't reach their ends.
Inputs may be any that keep to these rules, and one draw needn't show every extreme that they name: `token_place`: A permutation. Place s lies in group s // 1024 and is held by the device with dp index s // 1024 and grp index (s // 128) % 8; every token keeps its grp index. The tokens of one device go to exactly 16 dp indices, exactly 8 to each. `clip_index`: in each row, clips are runs of places numbered in order, each of 1 to 768 places.
All inputs are finite; a program needn't handle non-finite values.
Results may differ from the reference program's by a relative error of at most 0.015.
Values may be sent and summed in bfloat16 or wider, within the bound.
No kernel may reach another device: no remote copies, remote signals or barrier semaphores. Data moves between devices by JAX's collectives and lax.ppermute only.
A program may use at most 128 MiB of HBM per device.

```python
import math
import jax
import jax.numpy as jnp
import numpy as np
from jax import lax

HEADS = 16
HEAD_DIM = 128
ROPE_T = 16
TOK_DEV = 128
CLIPS = 2
QKV_W = 2048
GROUP_TOK = 1024
TOKENS = 32768
PIECES = 16
CAP = 8
N_DP = 32
N_GRP = 8


def draw_token_place(key, part):
    key = jax.random.fold_in(key, 7)
    subkeys = jax.random.split(key, 4)
    tau_table = jax.vmap(lambda subkey: jax.random.permutation(subkey, N_DP))(jax.random.split(subkeys[0], N_GRP))
    offsets = jax.vmap(lambda subkey: jax.random.permutation(subkey, N_DP)[:PIECES])(jax.random.split(subkeys[1], N_GRP))
    piece_order = jax.vmap(lambda subkey: jax.random.permutation(subkey, PIECES))(jax.random.split(subkeys[2], N_GRP))
    row_order = jax.vmap(lambda subkey: jax.random.permutation(subkey, TOK_DEV))(jax.random.split(subkeys[3], N_DP * N_GRP))
    row_order = row_order.reshape(N_DP, N_GRP, TOK_DEV)
    piece_index = row_order // CAP
    within = row_order % CAP
    dp_index = jnp.arange(N_DP, dtype=jnp.int32)[:, None, None]
    grp_index = jnp.arange(N_GRP, dtype=jnp.int32)[None, :, None]
    target = (tau_table[grp_index, dp_index] + offsets[grp_index, piece_index]) % N_DP
    slot_index = target * GROUP_TOK + grp_index * TOK_DEV + piece_order[grp_index, piece_index] * CAP + within
    return slot_index.reshape(-1).astype(jnp.int32)


def place_ends(values, own_key, low, largest):
    shape = values.shape
    spot = [jax.random.randint(jax.random.fold_in(own_key, axis), (), 0, shape[axis]) for axis in range(len(shape))]
    values = values.at[tuple(spot)].set(low)
    longest = shape.index(max(shape))
    spot[longest] = (spot[longest] + 1) % shape[longest]
    return values.at[tuple(spot)].set(largest)


def steps_of(stream_key, shape, cuts, smallest, largest):
    loudness = 1.0
    for dim, parts in cuts:
        steps = jax.random.uniform(jax.random.fold_in(jax.random.fold_in(stream_key, 6), dim), (parts,), jnp.float32, smallest / len(cuts), largest / len(cuts))
        loudness = loudness * jnp.repeat(jnp.exp(steps), shape[dim] // parts).reshape((-1,) + (1,) * (len(shape) - 1 - dim))
    return loudness


def split_up(amount, total, reach, lean):
    loads = [(1 << 20) // math.isqrt(rank ** lean) + 1 for rank in range(2, amount + 1)]
    rest, holding = total - reach - (amount - 1), [1] * (amount - 1)
    while rest > 0:
        candidates = [i for i in range(amount - 1) if holding[i] < reach]
        whole, budget = sum([loads[i] for i in candidates]), rest
        for i in candidates:
            extra = min(reach - holding[i], max(1, budget * loads[i] // whole), rest)
            holding[i] = holding[i] + extra
            rest = rest - extra
    return np.array([reach] + holding)


def uneven(key, amount, total, reach, slope):
    if amount == 2:
        one = jax.random.randint(key, (), max(1, total - reach), min(reach, total - 1) + 1)
        return jnp.stack([one, total - one])
    sizes = jnp.asarray(split_up(amount, total, reach, slope), jnp.int32)
    pairs = (amount - 1) // 2
    giver, taker = sizes[1:1 + 2 * pairs:2], sizes[2:2 + 2 * pairs:2]
    room = jnp.minimum(giver - 1, reach - taker)
    moved = jax.random.randint(jax.random.fold_in(key, 1), (pairs,), 0, 1 << 20) % (room + 1)
    sizes = sizes.at[1:1 + 2 * pairs:2].set(giver - moved).at[2:2 + 2 * pairs:2].set(taker + moved)
    return sizes[jax.random.permutation(jax.random.fold_in(key, 2), amount)]


def noise(own_key, dims, deviation, limit, cuts=(), kind=jnp.bfloat16):
    entries = jax.random.normal(own_key, dims, jnp.float32) * deviation
    if len(cuts) > 0:
        entries = steps_of(own_key, dims, cuts, -0.22, 0.18) * entries
    return jnp.clip(entries, min=-limit, max=limit).astype(kind)


def setup_inputs(seed: int = 0) -> dict:
    seeds = jax.random.split(jax.random.key(seed), 10)
    query_in = noise(seeds[0], (TOKENS, QKV_W), 1.0, 6.0, ((0, 256),))
    key_in = noise(seeds[1], (TOKENS, QKV_W), 1.0, 6.0, ((0, 256),))
    value_in = noise(seeds[2], (TOKENS, QKV_W), 1.0, 6.0, ((0, 256),))
    out_grad = noise(seeds[3], (TOKENS, QKV_W), 1.0, 6.0, ((0, 256),))
    query_gain = jnp.clip(jax.random.uniform(seeds[4], (HEAD_DIM,), jnp.float32, 1.5, 2.5), 1.5, 2.5)
    key_gain = jnp.clip(jax.random.uniform(seeds[5], (HEAD_DIM,), jnp.float32, 1.5, 2.5), 1.5, 2.5)
    positions = place_ends(jax.random.randint(seeds[6], (3, TOKENS), 0, 64), jax.random.fold_in(seeds[6], 1), 0, 63).astype(jnp.int32)
    token_place = draw_token_place(jax.random.fold_in(seeds[9], 71), 0)
    clip_index = jax.vmap(lambda own: jnp.searchsorted(jnp.cumsum(uneven(own, CLIPS, GROUP_TOK, GROUP_TOK * 3 // 4, 1)), jnp.arange(GROUP_TOK), side="right"))(jax.random.split(seeds[8], N_DP)).reshape((N_DP, GROUP_TOK)).astype(jnp.int32)
    return dict(query_in=query_in, key_in=key_in, value_in=value_in, out_grad=out_grad, query_gain=query_gain, key_gain=key_gain, positions=positions, token_place=token_place, clip_index=clip_index)


eps = 1e-06
rope_base = 256.0

def angle_table(positions, head_dim):
    half_dim = head_dim // 2
    time_pairs = ROPE_T // 2
    space_pairs = (head_dim - ROPE_T) // 4
    pair_index = jnp.arange(half_dim, dtype=jnp.int32)
    axis_of_pair = jnp.where(pair_index < time_pairs, 0, jnp.where(pair_index < time_pairs + space_pairs, 1, 2)).astype(jnp.int32)
    offset = jnp.where(axis_of_pair == 0, 0, jnp.where(axis_of_pair == 1, time_pairs, time_pairs + space_pairs)).astype(jnp.int32)
    span_dim = jnp.where(axis_of_pair == 0, ROPE_T, (head_dim - ROPE_T) // 2).astype(jnp.float32)
    frequency = jnp.power(jnp.float32(rope_base), -2.0 * (pair_index - offset).astype(jnp.float32) / span_dim)
    coordinates = positions.astype(jnp.float32)
    chosen = (axis_of_pair == 0).astype(jnp.float32)[None, :] * coordinates[0][:, None]
    chosen = chosen + (axis_of_pair == 1).astype(jnp.float32)[None, :] * coordinates[1][:, None]
    chosen = chosen + (axis_of_pair == 2).astype(jnp.float32)[None, :] * coordinates[2][:, None]
    return chosen * frequency[None, :]

def norm_rope(values, gain, cosine, sine):
    factor = lax.rsqrt(lax.optimization_barrier(jnp.mean(values * values, axis=-1, keepdims=True)) + eps)
    normed = values * factor * gain
    shaped = normed.reshape(normed.shape[:-1] + (normed.shape[-1] // 2, 2))
    first = shaped[..., 0]
    second = shaped[..., 1]
    cos_rows = cosine[:, None, :]
    sin_rows = sine[:, None, :]
    rotated = jnp.stack((first * cos_rows - second * sin_rows, second * cos_rows + first * sin_rows), axis=-1)
    return rotated.reshape(normed.shape)

def forward_group(query_rows, key_rows, value_rows, clip_row, factor):
    rows, heads, dim = query_rows.shape
    block = min(512, rows)
    count = rows // block
    key_f = key_rows.astype(jnp.float32)
    value_f = value_rows.astype(jnp.float32)

    def one_block(members):
        query_block, clip_block = members
        scores = jnp.einsum('qhd,khd->hqk', query_block.astype(jnp.float32), key_f) * factor
        same_clip = clip_block[:, None] == clip_row[None, :]
        raised = jnp.where(same_clip[None, :, :], jnp.exp(scores), 0.0)
        weights = raised / lax.optimization_barrier(jnp.sum(raised, axis=-1, keepdims=True))
        rounded = weights.astype(jnp.bfloat16)
        output = jnp.einsum('hqk,khd->qhd', rounded.astype(jnp.float32), value_f).astype(jnp.bfloat16)
        return (output, weights)
    outputs, weights = lax.map(one_block, (query_rows.reshape(count, block, heads, dim), clip_row.reshape(count, block)))
    return (outputs.reshape(rows, heads, dim), weights)

def backward_group(query_rows, key_rows, value_rows, output, grad_rows, weights, factor):
    rows, heads, dim = query_rows.shape
    block = min(512, rows)
    count = rows // block
    key_f = key_rows.astype(jnp.float32)
    value_f = value_rows.astype(jnp.float32)
    grad_f = grad_rows.astype(jnp.float32)
    row_dot = lax.optimization_barrier(jnp.sum(grad_f * output.astype(jnp.float32), axis=-1))

    def one_block(carry, members):
        value_acc, key_acc = carry
        query_block, grad_block, dot_block, weight_block = members
        rounded = weight_block.astype(jnp.bfloat16)
        value_acc = value_acc + jnp.einsum('hqk,qhd->khd', rounded.astype(jnp.float32), grad_block)
        grad_weights = jnp.einsum('qhd,khd->hqk', grad_block, value_f)
        grad_scores = (weight_block * (grad_weights - dot_block.T[:, :, None])).astype(jnp.bfloat16)
        grad_query = (jnp.einsum('hqk,khd->qhd', grad_scores.astype(jnp.float32), key_f) * factor).astype(jnp.bfloat16)
        key_acc = key_acc + jnp.einsum('hqk,qhd->khd', grad_scores.astype(jnp.float32), query_block.astype(jnp.float32))
        return ((value_acc, key_acc), grad_query)
    zeros = jnp.zeros((rows, heads, dim), jnp.float32)
    members = (query_rows.reshape(count, block, heads, dim), grad_f.reshape(count, block, heads, dim), row_dot.reshape(count, block, heads), weights)
    (value_acc, key_acc), grad_query = lax.scan(one_block, (zeros, zeros), members)
    return (grad_query.reshape(rows, heads, dim), (key_acc * factor).astype(jnp.bfloat16), value_acc.astype(jnp.bfloat16))

def reference(query_in, key_in, value_in, out_grad, query_gain, key_gain, positions, token_place, clip_index):
    factor = 1.0 / math.sqrt(HEAD_DIM)
    angles = angle_table(positions, HEAD_DIM)
    cosine = jnp.cos(angles)
    sine = jnp.sin(angles)

    def prepare_query(values):
        return norm_rope(values, query_gain, cosine, sine)

    def prepare_key(values):
        return norm_rope(values, key_gain, cosine, sine)
    query_f = query_in.astype(jnp.float32).reshape(TOKENS, HEADS, HEAD_DIM)
    key_f = key_in.astype(jnp.float32).reshape(TOKENS, HEADS, HEAD_DIM)
    query_ready, query_pull = jax.vjp(prepare_query, query_f)
    key_ready, key_pull = jax.vjp(prepare_key, key_f)
    query_ready = query_ready.astype(jnp.bfloat16)
    key_ready = key_ready.astype(jnp.bfloat16)

    def to_groups(array):
        shaped = array.reshape(TOKENS, HEADS, HEAD_DIM)
        placed = jnp.zeros_like(shaped).at[token_place].set(shaped)
        return placed.reshape(N_DP, GROUP_TOK, HEADS, HEAD_DIM)

    def to_loader(array):
        return array.reshape(TOKENS, HEADS, HEAD_DIM)[token_place]

    def per_group(members):
        query_rows, key_rows, value_rows, grad_rows, clip_row = members
        output, weights = forward_group(query_rows, key_rows, value_rows, clip_row, factor)
        grad_query, grad_key, grad_value = backward_group(query_rows, key_rows, value_rows, output, grad_rows, weights, factor)
        return (output, grad_query, grad_key, grad_value)
    outputs = lax.map(per_group, (to_groups(query_ready), to_groups(key_ready), to_groups(value_in), to_groups(out_grad), clip_index))
    attention = to_loader(outputs[0]).reshape(TOKENS, QKV_W)
    grad_qready = to_loader(outputs[1]).astype(jnp.float32)
    grad_kready = to_loader(outputs[2]).astype(jnp.float32)
    grad_value = to_loader(outputs[3]).reshape(TOKENS, QKV_W)
    grad_query = query_pull(grad_qready)[0].astype(jnp.bfloat16).reshape(TOKENS, QKV_W)
    grad_key = key_pull(grad_kready)[0].astype(jnp.bfloat16).reshape(TOKENS, QKV_W)
    return (attention, grad_query, grad_key, grad_value)
```

```python
import functools
import math

import jax
import jax.numpy as jnp
from jax import lax
from jax.experimental import pallas as pl
from jax.experimental.pallas import tpu as pltpu
from jax.sharding import PartitionSpec as P

HEAD_DIM = 128
ROPE_T = 16
CAP = 8
META = 128
eps = 1e-06
rope_base = 256.0
factor = 1.0 / math.sqrt(HEAD_DIM)
MB = 1024 * 1024


def f32_dot(a, b, dims):
    return lax.dot_general(a, b, (dims, ((), ())), preferred_element_type=jnp.float32)


def as_column(row):
    n = row.shape[1]
    eye = lax.broadcasted_iota(jnp.int32, (n, n), 0) == lax.broadcasted_iota(jnp.int32, (n, n), 1)
    return jnp.sum(jnp.where(eye, jnp.broadcast_to(row, (n, n)), 0.0), axis=1, keepdims=True)


def slot_of_token(place_row, group_rows):
    n = place_row.shape[1]
    target = (place_row // group_rows).astype(jnp.float32)
    column = as_column(target)
    earlier = lax.broadcasted_iota(jnp.int32, (n, n), 0) < lax.broadcasted_iota(
        jnp.int32, (n, n), 1
    )
    same = (column == jnp.broadcast_to(target, (n, n))) & earlier
    rank = jnp.sum(jnp.where(same, 1.0, 0.0), axis=0, keepdims=True)
    return target * CAP + rank


def rotation(positions):
    n = positions.shape[1]
    channel = lax.broadcasted_iota(jnp.int32, (1, HEAD_DIM), 1)
    pair = channel // 2
    time_pairs = ROPE_T // 2
    space_pairs = (HEAD_DIM - ROPE_T) // 4
    first = pair < time_pairs
    second = pair < time_pairs + space_pairs
    offset = jnp.where(first, 0, jnp.where(second, time_pairs, time_pairs + space_pairs))
    span = jnp.where(first, float(ROPE_T), float((HEAD_DIM - ROPE_T) // 2))
    frequency = jnp.exp(
        (-2.0 * math.log(rope_base)) * (pair - offset).astype(jnp.float32) / span
    )
    rows = positions.astype(jnp.float32)
    shape = (n, HEAD_DIM)
    columns = [jnp.broadcast_to(as_column(rows[i : i + 1]), shape) for i in range(3)]
    chosen = jnp.where(first, columns[0], jnp.where(second, columns[1], columns[2]))
    angles = chosen * frequency
    sine = jnp.sin(angles)
    odd = (channel % 2) == 1
    return jnp.cos(angles), jnp.where(odd, sine, -sine)


def swap_pairs(values):
    odd = (lax.broadcasted_iota(jnp.int32, values.shape, 1) % 2) == 1
    down = pltpu.roll(values, 1, axis=1)
    up = pltpu.roll(values, HEAD_DIM - 1, axis=1)
    return jnp.where(odd, down, up)


def norm_factor(values):
    return lax.rsqrt(jnp.mean(values * values, axis=-1, keepdims=True) + eps)


def pack_kernel(
    group_rows,
    query_ref,
    key_ref,
    value_ref,
    grad_ref,
    query_gain_ref,
    key_gain_ref,
    positions_ref,
    place_ref,
    out_ref,
    cosine_ref,
    sine_ref,
    pick_ref,
    meta_ref,
):
    slots = pick_ref.shape[0]
    n = query_ref.shape[0]
    dp_count = slots // CAP

    @pl.when(pl.program_id(0) == 0)
    def _():
        cosine, sine = rotation(positions_ref[...])
        cosine_ref[...] = cosine
        sine_ref[...] = sine
        place = place_ref[...]
        slot = slot_of_token(place, group_rows).astype(jnp.int32)
        pick = lax.broadcasted_iota(jnp.int32, (slots, n), 0) == jnp.broadcast_to(slot, (slots, n))
        pick = jnp.where(pick, 1.0, 0.0).astype(jnp.bfloat16)
        pick_ref[...] = pick
        code = jnp.broadcast_to((place % n + 1).astype(jnp.float32), (META, n))
        meta = f32_dot(pick, code.astype(jnp.bfloat16), ((1,), (1,)))
        meta_ref[...] = meta.reshape(dp_count, CAP, META)

    pick = pick_ref[...]
    width = query_ref.shape[1]

    def prepared(ref, gain_ref):
        parts = []
        for start in range(0, width, HEAD_DIM):
            values = ref[:, start : start + HEAD_DIM].astype(jnp.float32)
            normed = values * norm_factor(values) * gain_ref[...]
            rotated = normed * cosine_ref[...] + swap_pairs(normed) * sine_ref[...]
            parts.append(rotated.astype(jnp.bfloat16))
        return jnp.concatenate(parts, axis=1)

    def put(index, rows):
        packed = f32_dot(pick, rows, ((1,), (0,))).reshape(dp_count, CAP, width)
        out_ref[:, 0, :, index * width : (index + 1) * width] = packed.astype(jnp.bfloat16)

    put(0, prepared(query_ref, query_gain_ref))
    put(1, prepared(key_ref, key_gain_ref))
    put(2, value_ref[...])
    put(3, grad_ref[...])
    out_ref[:, 0, :, 4 * width :] = meta_ref[...].astype(jnp.bfloat16)


def attend_kernel(
    arrived_ref, clip_ref, out_ref, query_ref, key_ref, value_ref, grad_ref, pick_ref, result_ref,
    key_acc, value_acc
):
    dp_count, grp_count, cap, columns = arrived_ref.shape
    rows, width = query_ref.shape
    slots = dp_count * cap
    own = rows // grp_count
    block = 256

    for g in range(grp_count):
        code = arrived_ref[:, g, :, 4 * width :].astype(jnp.float32).reshape(slots, META)
        spot = lax.broadcasted_iota(jnp.int32, (slots, own), 1) + 1
        pick = jnp.where(code == spot.astype(jnp.float32), 1.0, 0.0).astype(jnp.bfloat16)
        pick_ref[g] = pick
        for index, target in enumerate((query_ref, key_ref, value_ref, grad_ref)):
            held = arrived_ref[:, g, :, index * width : (index + 1) * width]
            held = held.astype(jnp.float32).reshape(slots, width).astype(jnp.bfloat16)
            target[g * own : (g + 1) * own, :] = f32_dot(pick, held, ((0,), (0,))).astype(
                jnp.bfloat16
            )

    is_first = (clip_ref[...] == 0).astype(jnp.float32)
    first_rows = jnp.sum(is_first, axis=1, keepdims=True)
    key_place = lax.broadcasted_iota(jnp.int32, (1, rows), 1).astype(jnp.float32)
    key_second = key_place >= first_rows

    for head in range(width // HEAD_DIM):
        lanes = slice(head * HEAD_DIM, (head + 1) * HEAD_DIM)
        key = key_ref[:, lanes]
        value = value_ref[:, lanes]
        for start in range(0, rows, block):
            part = slice(start, start + block)
            query = query_ref[part, lanes]
            grad = grad_ref[part, lanes]
            scores = f32_dot(query, key, ((1,), (1,)))
            raised = jnp.exp2(scores * (factor * math.log2(math.e)))
            place = lax.broadcasted_iota(jnp.int32, (block, 1), 0).astype(jnp.float32) + start
            second = place >= first_rows
            raised = jnp.where(second == key_second, raised, 0.0)
            weights = raised * (1.0 / jnp.sum(raised, axis=1, keepdims=True))
            weights_low = weights.astype(jnp.bfloat16)
            attended = f32_dot(weights_low, value, ((1,), (0,))).astype(jnp.bfloat16)
            result_ref[0, part, lanes] = attended
            row_dot = jnp.sum(
                grad.astype(jnp.float32) * attended.astype(jnp.float32), axis=1, keepdims=True
            )
            grad_weights = f32_dot(grad, value, ((1,), (1,)))
            grad_scores = (weights * (grad_weights - row_dot)).astype(jnp.bfloat16)
            grad_query = f32_dot(grad_scores, key, ((1,), (0,))) * factor
            result_ref[1, part, lanes] = grad_query.astype(jnp.bfloat16)
            key_part = f32_dot(grad_scores, query, ((0,), (0,)))
            value_part = f32_dot(weights_low, grad, ((0,), (0,)))
            if start == 0:
                key_acc[...] = key_part
                value_acc[...] = value_part
            else:
                key_acc[...] += key_part
                value_acc[...] += value_part
        result_ref[2, :, lanes] = (key_acc[...] * factor).astype(jnp.bfloat16)
        result_ref[3, :, lanes] = value_acc[...].astype(jnp.bfloat16)

    for g in range(grp_count):
        pick = pick_ref[g]
        for index in range(4):
            held = result_ref[index, g * own : (g + 1) * own, :]
            packed = f32_dot(pick, held, ((1,), (0,))).reshape(dp_count, cap, width)
            out_ref[:, g, :, index * width : (index + 1) * width] = packed.astype(jnp.bfloat16)


def unpack_kernel(
    group_rows,
    back_ref,
    query_ref,
    key_ref,
    query_gain_ref,
    key_gain_ref,
    positions_ref,
    place_ref,
    attention_ref,
    grad_query_ref,
    grad_key_ref,
    grad_value_ref,
    cosine_ref,
    sine_ref,
    pick_ref,
):
    dp_count, _, cap, _ = back_ref.shape
    n, width = query_ref.shape
    slots = dp_count * cap

    @pl.when(pl.program_id(0) == 0)
    def _():
        cosine, sine = rotation(positions_ref[...])
        cosine_ref[...] = cosine
        sine_ref[...] = sine
        slot = as_column(slot_of_token(place_ref[...], group_rows)).astype(jnp.int32)
        pick = jnp.broadcast_to(slot, (n, slots)) == lax.broadcasted_iota(jnp.int32, (n, slots), 1)
        pick_ref[...] = jnp.where(pick, 1.0, 0.0).astype(jnp.bfloat16)

    pick = pick_ref[...]

    def take(index):
        held = back_ref[:, 0, :, index * width : (index + 1) * width]
        held = held.astype(jnp.float32).reshape(slots, width).astype(jnp.bfloat16)
        return f32_dot(pick, held, ((1,), (0,)))

    def pulled(index, ref, gain_ref, out_ref):
        grads = take(index)
        for start in range(0, width, HEAD_DIM):
            lanes = slice(start, start + HEAD_DIM)
            values = ref[:, lanes].astype(jnp.float32)
            scale = norm_factor(values)
            grad = grads[:, lanes]
            grad = grad * cosine_ref[...] - swap_pairs(grad) * sine_ref[...]
            grad = grad * gain_ref[...]
            unit = values * scale
            along = jnp.mean(grad * unit, axis=-1, keepdims=True)
            out_ref[:, lanes] = (scale * (grad - unit * along)).astype(jnp.bfloat16)

    attention_ref[...] = take(0).astype(jnp.bfloat16)
    grad_value_ref[...] = take(3).astype(jnp.bfloat16)
    pulled(1, query_ref, query_gain_ref, grad_query_ref)
    pulled(2, key_ref, key_gain_ref, grad_key_ref)


def on_device(
    query_in, key_in, value_in, out_grad, query_gain, key_gain, positions, token_place, clip_index
):
    n, width = query_in.shape
    dp_count = lax.axis_size("dp")
    grp_count = lax.axis_size("grp")
    group_rows = n * grp_count
    slots = dp_count * CAP
    narrow = width // grp_count
    query_gain = query_gain.reshape(1, HEAD_DIM)
    key_gain = key_gain.reshape(1, HEAD_DIM)
    place = token_place.reshape(1, n)
    bf16 = jnp.bfloat16

    def whole(array):
        return pl.BlockSpec(array.shape, lambda h: (0,) * array.ndim)

    slab = pl.BlockSpec((n, narrow), lambda h: (0, h))
    sent_width = 4 * narrow + META
    small = (query_gain, key_gain, positions, place)
    turn = [pltpu.VMEM((n, HEAD_DIM), jnp.float32)] * 2

    packed = pl.pallas_call(
        functools.partial(pack_kernel, group_rows),
        name="pack",
        grid=(grp_count,),
        in_specs=[slab] * 4 + [whole(a) for a in small],
        out_specs=pl.BlockSpec((dp_count, 1, CAP, sent_width), lambda h: (0, h, 0, 0)),
        out_shape=jax.ShapeDtypeStruct((dp_count, grp_count, CAP, sent_width), bf16),
        scratch_shapes=turn
        + [pltpu.VMEM((slots, n), bf16), pltpu.VMEM((dp_count, CAP, META), jnp.float32)],
        compiler_params=pltpu.CompilerParams(vmem_limit_bytes=24 * MB),
    )(query_in, key_in, value_in, out_grad, *small)

    def exchange(array):
        flat = array.reshape((dp_count * grp_count,) + array.shape[2:])
        moved = lax.all_to_all(flat, ("dp", "grp"), split_axis=0, concat_axis=0, tiled=True)
        return moved.reshape(array.shape)

    arrived = exchange(packed)
    results = pl.pallas_call(
        attend_kernel,
        name="attend",
        out_shape=jax.ShapeDtypeStruct((dp_count, grp_count, CAP, 4 * narrow), bf16),
        scratch_shapes=[pltpu.VMEM((group_rows, narrow), bf16)] * 4
        + [
            pltpu.VMEM((grp_count, slots, n), bf16),
            pltpu.VMEM((4, group_rows, narrow), bf16),
            pltpu.VMEM((group_rows, HEAD_DIM), jnp.float32),
            pltpu.VMEM((group_rows, HEAD_DIM), jnp.float32),
        ],
        compiler_params=pltpu.CompilerParams(vmem_limit_bytes=40 * MB),
    )(arrived, clip_index)
    back = exchange(results)

    return pl.pallas_call(
        functools.partial(unpack_kernel, group_rows),
        name="unpack",
        grid=(grp_count,),
        in_specs=[pl.BlockSpec((dp_count, 1, CAP, 4 * narrow), lambda h: (0, h, 0, 0))]
        + [slab] * 2
        + [whole(a) for a in small],
        out_specs=[slab] * 4,
        out_shape=[jax.ShapeDtypeStruct((n, width), bf16)] * 4,
        scratch_shapes=turn + [pltpu.VMEM((n, slots), bf16)],
        compiler_params=pltpu.CompilerParams(vmem_limit_bytes=24 * MB),
    )(back, query_in, key_in, *small)


def solution(mesh):
    rows = P(("dp", "grp"), None)
    in_specs = (
        rows,
        rows,
        rows,
        rows,
        P(),
        P(),
        P(None, ("dp", "grp")),
        P(("dp", "grp")),
        P("dp", None),
    )

    def run(*arrays):
        return tuple(on_device(*arrays))

    return jax.shard_map(
        run, mesh=mesh, in_specs=in_specs, out_specs=(rows,) * 4, check_vma=False
    )
```

```python
import functools
import math

import jax
import jax.numpy as jnp
from jax import lax
from jax.experimental import pallas as pl
from jax.experimental.pallas import tpu as pltpu
from jax.sharding import PartitionSpec as P

HEAD_DIM = 128
ROPE_T = 16
CAP = 8
META = 128
eps = 1e-06
rope_base = 256.0
factor = 1.0 / math.sqrt(HEAD_DIM)
MB = 1024 * 1024


def f32_dot(a, b, dims):
    return lax.dot_general(a, b, (dims, ((), ())), preferred_element_type=jnp.float32)


def as_column(row):
    n = row.shape[1]
    eye = lax.broadcasted_iota(jnp.int32, (n, n), 0) == lax.broadcasted_iota(jnp.int32, (n, n), 1)
    return jnp.sum(jnp.where(eye, jnp.broadcast_to(row, (n, n)), 0.0), axis=1, keepdims=True)


def slot_of_token(place_row, group_rows):
    n = place_row.shape[1]
    target = (place_row // group_rows).astype(jnp.float32)
    column = as_column(target)
    earlier = lax.broadcasted_iota(jnp.int32, (n, n), 0) < lax.broadcasted_iota(
        jnp.int32, (n, n), 1
    )
    same = (column == jnp.broadcast_to(target, (n, n))) & earlier
    rank = jnp.sum(jnp.where(same, 1.0, 0.0), axis=0, keepdims=True)
    return target * CAP + rank


def rotation(positions):
    n = positions.shape[1]
    channel = lax.broadcasted_iota(jnp.int32, (1, HEAD_DIM), 1)
    pair = channel // 2
    time_pairs = ROPE_T // 2
    space_pairs = (HEAD_DIM - ROPE_T) // 4
    first = pair < time_pairs
    second = pair < time_pairs + space_pairs
    offset = jnp.where(first, 0, jnp.where(second, time_pairs, time_pairs + space_pairs))
    span = jnp.where(first, float(ROPE_T), float((HEAD_DIM - ROPE_T) // 2))
    frequency = jnp.exp(
        (-2.0 * math.log(rope_base)) * (pair - offset).astype(jnp.float32) / span
    )
    rows = positions.astype(jnp.float32)
    shape = (n, HEAD_DIM)
    columns = [jnp.broadcast_to(as_column(rows[i : i + 1]), shape) for i in range(3)]
    chosen = jnp.where(first, columns[0], jnp.where(second, columns[1], columns[2]))
    angles = chosen * frequency
    sine = jnp.sin(angles)
    odd = (channel % 2) == 1
    return jnp.cos(angles), jnp.where(odd, sine, -sine)


def swap_matrix(size):
    row = lax.broadcasted_iota(jnp.int32, (size, size), 0)
    column = lax.broadcasted_iota(jnp.int32, (size, size), 1)
    return jnp.where((row ^ 1) == column, 1.0, 0.0).astype(jnp.bfloat16)


def swapped_gain(gain):
    rows = jnp.broadcast_to(gain, (8, HEAD_DIM))
    odd = (lax.broadcasted_iota(jnp.int32, rows.shape, 1) % 2) == 1
    down = pltpu.roll(rows, 1, axis=1)
    up = pltpu.roll(rows, HEAD_DIM - 1, axis=1)
    return jnp.where(odd, down, up)[0:1]


def norm_factor(values):
    return lax.rsqrt(jnp.mean(values * values, axis=-1, keepdims=True) + eps)


def pack_kernel(group_rows, *refs):
    sources, out_ref, held = refs[:8], refs[8], refs[9:17]
    sent_ref, pick_ref, meta_ref, sems, out_sems = refs[17:]
    copies = [
        pltpu.make_async_copy(source, target, sems.at[i])
        for i, (source, target) in enumerate(zip(sources, held))
    ]
    for i in (7, 6, 4, 5, 0, 1, 2, 3):
        copies[i].start()
    query_ref, key_ref, value_ref, grad_ref = held[:4]
    query_gain_ref, key_gain_ref, positions_ref, place_ref = held[4:]
    slots, n = pick_ref.shape
    grp_count = out_ref.shape[0]
    narrow = query_ref.shape[1] // grp_count

    copies[7].wait()
    place = place_ref[...]
    slot = slot_of_token(place, group_rows).astype(jnp.int32)
    pick = lax.broadcasted_iota(jnp.int32, (slots, n), 0) == jnp.broadcast_to(slot, (slots, n))
    pick_ref[...] = jnp.where(pick, 1.0, 0.0).astype(jnp.bfloat16)
    code = jnp.broadcast_to((place % n + 1).astype(jnp.float32), (META, n)).astype(jnp.bfloat16)
    meta_ref[...] = f32_dot(pick_ref[...], code, ((1,), (1,))).astype(jnp.bfloat16)
    copies[6].wait()
    cosine, sine = rotation(positions_ref[...])
    swap = swap_matrix(narrow)
    copies[4].wait()
    copies[5].wait()
    turns = [
        (gain_ref[...] * cosine, swapped_gain(gain_ref[...]) * sine)
        for gain_ref in (query_gain_ref, key_gain_ref)
    ]
    for i in (0, 1, 2, 3):
        copies[i].wait()

    sends = []
    for h in range(grp_count):
        block = slice(h * narrow, (h + 1) * narrow)
        parts = []
        for ref, (along, across) in zip((query_ref, key_ref), turns):
            rows = ref[:, block]
            other = f32_dot(rows, swap, ((1,), (0,)))
            for start in range(0, narrow, HEAD_DIM):
                lanes = slice(start, start + HEAD_DIM)
                values = rows[:, lanes].astype(jnp.float32)
                rotated = (values * along + other[:, lanes] * across) * norm_factor(values)
                parts.append(rotated.astype(jnp.bfloat16))
        rows = jnp.concatenate(parts + [value_ref[:, block], grad_ref[:, block]], axis=1)
        sent_ref[h, :, : 4 * narrow] = f32_dot(pick_ref[...], rows, ((1,), (0,))).astype(
            jnp.bfloat16
        )
        sent_ref[h, :, 4 * narrow :] = meta_ref[...]
        sends.append(pltpu.make_async_copy(sent_ref.at[h], out_ref.at[h], out_sems.at[h]))
        sends[-1].start()
    for send in sends:
        send.wait()


def attend_kernel(
    arrived_ref,
    clip_ref,
    out_ref,
    token_ref,
    pick_ref,
    query_clip_ref,
    key_clip_ref,
    weights_ref,
    scores_ref,
    by_query_ref,
    by_key_ref,
):
    grp_count, slots, _ = arrived_ref.shape
    rows, columns = token_ref.shape
    width = columns // 4
    own = rows // grp_count
    block = rows // 4
    bf16 = jnp.bfloat16

    for g in range(grp_count):
        code = arrived_ref[g, :, columns:].astype(jnp.float32)
        spot = lax.broadcasted_iota(jnp.int32, (slots, own), 1) + 1
        pick = jnp.where(code == spot.astype(jnp.float32), 1.0, 0.0).astype(bf16)
        pick_ref[g] = pick
        token_ref[g * own : (g + 1) * own, :] = f32_dot(
            pick, arrived_ref[g, :, :columns], ((0,), (0,))
        ).astype(bf16)

    first_rows = jnp.sum((clip_ref[...] == 0).astype(jnp.float32), axis=1, keepdims=True)
    place = lax.broadcasted_iota(jnp.int32, (rows, HEAD_DIM), 0).astype(jnp.float32)
    channel = lax.broadcasted_iota(jnp.int32, (rows, HEAD_DIM), 1)
    clip = jnp.where(place >= first_rows, 1, 0)
    query_clip_ref[...] = jnp.where(channel == clip, 1.0, 0.0).astype(bf16)
    key_clip_ref[...] = jnp.where(channel == 1 - clip, -4096.0, 0.0).astype(bf16)

    spans = [(0, 3 * block), (0, rows), (0, rows), (block, rows)]
    for head in range(width // HEAD_DIM):
        at = [slice(a * width + head * HEAD_DIM, a * width + (head + 1) * HEAD_DIM) for a in range(4)]
        for i, (low, high) in enumerate(spans):
            part = slice(i * block, (i + 1) * block)
            query = token_ref[part, at[0]]
            key = token_ref[low:high, at[1]]
            value = token_ref[low:high, at[2]]
            grad = token_ref[part, at[3]]
            scores = f32_dot(
                jnp.concatenate([query, query_clip_ref[part, :]], axis=1),
                jnp.concatenate([key, key_clip_ref[low:high, :]], axis=1),
                ((1,), (1,)),
            )
            raised = jnp.exp2(scores * (factor * math.log2(math.e)))
            weights = raised * (1.0 / jnp.sum(raised, axis=1, keepdims=True))
            weights_low = weights.astype(bf16)
            weights_ref[part, low:high] = weights_low
            attended = f32_dot(weights_low, value, ((1,), (0,))).astype(bf16)
            by_query_ref[part, head * HEAD_DIM : (head + 1) * HEAD_DIM] = attended
            row_dot = jnp.sum(
                grad.astype(jnp.float32) * attended.astype(jnp.float32), axis=1, keepdims=True
            )
            grad_weights = f32_dot(grad, value, ((1,), (1,)))
            grad_scores = (weights * (grad_weights - row_dot)).astype(bf16)
            scores_ref[part, low:high] = grad_scores
            grad_query = f32_dot(grad_scores, key, ((1,), (0,))) * factor
            by_query_ref[part, width + head * HEAD_DIM : width + (head + 1) * HEAD_DIM] = (
                grad_query.astype(bf16)
            )
        meets = [(0, block, 0, 3 * block), (block, 3 * block, 0, rows), (3 * block, rows, block, rows)]
        for low, high, first, last in meets:
            query = token_ref[first:last, at[0]]
            grad = token_ref[first:last, at[3]]
            channels = slice(head * HEAD_DIM, (head + 1) * HEAD_DIM)
            by_key_ref[0, channels, low:high] = (
                f32_dot(query, scores_ref[first:last, low:high], ((0,), (0,))) * factor
            ).astype(bf16)
            by_key_ref[1, channels, low:high] = f32_dot(
                grad, weights_ref[first:last, low:high], ((0,), (0,))
            ).astype(bf16)

    for g in range(grp_count):
        pick = pick_ref[g]
        part = slice(g * own, (g + 1) * own)
        out_ref[g, :, : 2 * width] = f32_dot(pick, by_query_ref[part, :], ((1,), (0,))).astype(bf16)
        for index in range(2):
            out_ref[g, :, (2 + index) * width : (3 + index) * width] = f32_dot(
                pick, by_key_ref[index, :, part], ((1,), (1,))
            ).astype(bf16)


def unpack_kernel(
    group_rows,
    back_ref,
    query_ref,
    key_ref,
    query_gain_ref,
    key_gain_ref,
    positions_ref,
    place_ref,
    *refs,
):
    outs, held, sems = refs[:4], refs[4:8], refs[8]
    grp_count, slots, _ = back_ref.shape
    n, width = query_ref.shape
    narrow = width // grp_count
    copies = [
        pltpu.make_async_copy(source, target, sems.at[i])
        for i, (source, target) in enumerate(zip(held, outs))
    ]
    slot = as_column(slot_of_token(place_ref[...], group_rows)).astype(jnp.int32)
    pick = jnp.broadcast_to(slot, (n, slots)) == lax.broadcasted_iota(jnp.int32, (n, slots), 1)
    pick = jnp.where(pick, 1.0, 0.0).astype(jnp.bfloat16)

    def take(h, index):
        rows = back_ref[h, :, index * narrow : (index + 1) * narrow]
        return f32_dot(pick, rows, ((1,), (0,)))

    for index, out in ((0, 0), (3, 3)):
        for h in range(grp_count):
            held[out][:, h * narrow : (h + 1) * narrow] = take(h, index).astype(jnp.bfloat16)
        copies[out].start()

    cosine, sine = rotation(positions_ref[...])
    swap = swap_matrix(narrow)
    for index, ref, gain_ref in ((1, query_ref, query_gain_ref), (2, key_ref, key_gain_ref)):
        along = cosine * gain_ref[...]
        across = sine * gain_ref[...]
        for h in range(grp_count):
            grads = take(h, index)
            other = f32_dot(grads.astype(jnp.bfloat16), swap, ((1,), (0,)))
            for start in range(0, narrow, HEAD_DIM):
                lanes = slice(h * narrow + start, h * narrow + start + HEAD_DIM)
                inner = slice(start, start + HEAD_DIM)
                values = ref[:, lanes].astype(jnp.float32)
                scale = norm_factor(values)
                grad = grads[:, inner] * along - other[:, inner] * across
                unit = values * scale
                share = jnp.mean(grad * unit, axis=-1, keepdims=True)
                held[index][:, lanes] = (scale * (grad - unit * share)).astype(jnp.bfloat16)
        copies[index].start()
    for copy in copies:
        copy.wait()


def on_device(
    query_in, key_in, value_in, out_grad, query_gain, key_gain, positions, token_place, clip_index
):
    n, width = query_in.shape
    dp_count = lax.axis_size("dp")
    grp_count = lax.axis_size("grp")
    group_rows = n * grp_count
    slots = dp_count * CAP
    narrow = width // grp_count
    query_gain = query_gain.reshape(1, HEAD_DIM)
    key_gain = key_gain.reshape(1, HEAD_DIM)
    place = token_place.reshape(1, n)
    bf16 = jnp.bfloat16
    vmem = pltpu.VMEM
    arguments = (query_in, key_in, value_in, out_grad, query_gain, key_gain, positions, place)
    in_hbm = pl.BlockSpec(memory_space=pltpu.HBM)
    sent_shape = (grp_count, slots, 4 * narrow + META)

    packed = pl.pallas_call(
        functools.partial(pack_kernel, group_rows),
        name="pack",
        in_specs=[in_hbm] * 8,
        out_specs=in_hbm,
        out_shape=jax.ShapeDtypeStruct(sent_shape, bf16),
        scratch_shapes=[vmem(a.shape, a.dtype) for a in arguments]
        + [
            vmem(sent_shape, bf16),
            vmem((slots, n), bf16),
            vmem((slots, META), bf16),
            pltpu.SemaphoreType.DMA((8,)),
            pltpu.SemaphoreType.DMA((grp_count,)),
        ],
        compiler_params=pltpu.CompilerParams(vmem_limit_bytes=60 * MB),
    )(*arguments)

    def exchange(array):
        flat = array.reshape(dp_count * grp_count, CAP, array.shape[2])
        moved = lax.all_to_all(flat, ("grp", "dp"), split_axis=0, concat_axis=0, tiled=True)
        return moved.reshape(array.shape)

    arrived = exchange(packed)
    results = pl.pallas_call(
        attend_kernel,
        name="attend",
        out_shape=jax.ShapeDtypeStruct((grp_count, slots, 4 * narrow), bf16),
        scratch_shapes=[
            vmem((group_rows, 4 * narrow), bf16),
            vmem((grp_count, slots, n), bf16),
            vmem((group_rows, HEAD_DIM), bf16),
            vmem((group_rows, HEAD_DIM), bf16),
            vmem((group_rows, group_rows), bf16),
            vmem((group_rows, group_rows), bf16),
            vmem((group_rows, 2 * narrow), bf16),
            vmem((2, narrow, group_rows), bf16),
        ],
        compiler_params=pltpu.CompilerParams(vmem_limit_bytes=40 * MB),
    )(arrived, clip_index)
    back = exchange(results)

    small = (query_gain, key_gain, positions, place)
    return pl.pallas_call(
        functools.partial(unpack_kernel, group_rows),
        name="unpack",
        out_specs=[in_hbm] * 4,
        out_shape=[jax.ShapeDtypeStruct((n, width), bf16)] * 4,
        scratch_shapes=[vmem((n, width), bf16)] * 4 + [pltpu.SemaphoreType.DMA((4,))],
        compiler_params=pltpu.CompilerParams(vmem_limit_bytes=24 * MB),
    )(back, query_in, key_in, *small)


def solution(mesh):
    rows = P(("dp", "grp"), None)
    in_specs = (
        rows,
        rows,
        rows,
        rows,
        P(),
        P(),
        P(None, ("dp", "grp")),
        P(("dp", "grp")),
        P("dp", None),
    )

    def run(*arrays):
        return tuple(on_device(*arrays))

    return jax.shard_map(
        run, mesh=mesh, in_specs=in_specs, out_specs=(rows,) * 4, check_vma=False
    )
```

```python
import functools
import math

import jax
import jax.numpy as jnp
from jax import lax
from jax.experimental import pallas as pl
from jax.experimental.pallas import tpu as pltpu
from jax.sharding import PartitionSpec as P

HEAD_DIM = 128
ROPE_T = 16
CAP = 8
Y_COUNT = 4
Z_COUNT = 8
eps = 1e-06
rope_base = 256.0
factor = 1.0 / math.sqrt(HEAD_DIM)
MB = 1024 * 1024


def f32_dot(a, b, dims):
    return lax.dot_general(a, b, (dims, ((), ())), preferred_element_type=jnp.float32)


def as_column(row):
    n = row.shape[1]
    eye = lax.broadcasted_iota(jnp.int32, (n, n), 0) == lax.broadcasted_iota(jnp.int32, (n, n), 1)
    return jnp.sum(jnp.where(eye, jnp.broadcast_to(row, (n, n)), 0.0), axis=1, keepdims=True)


def slot_of_token(place_row, group_rows):
    n = place_row.shape[1]
    target = (place_row // group_rows).astype(jnp.float32)
    column = as_column(target)
    earlier = lax.broadcasted_iota(jnp.int32, (n, n), 0) < lax.broadcasted_iota(
        jnp.int32, (n, n), 1
    )
    same = (column == jnp.broadcast_to(target, (n, n))) & earlier
    rank = jnp.sum(jnp.where(same, 1.0, 0.0), axis=0, keepdims=True)
    return target * CAP + rank


def rotation(positions):
    n = positions.shape[1]
    channel = lax.broadcasted_iota(jnp.int32, (1, HEAD_DIM), 1)
    pair = channel // 2
    time_pairs = ROPE_T // 2
    space_pairs = (HEAD_DIM - ROPE_T) // 4
    first = pair < time_pairs
    second = pair < time_pairs + space_pairs
    offset = jnp.where(first, 0, jnp.where(second, time_pairs, time_pairs + space_pairs))
    span = jnp.where(first, float(ROPE_T), float((HEAD_DIM - ROPE_T) // 2))
    frequency = jnp.exp(
        (-2.0 * math.log(rope_base)) * (pair - offset).astype(jnp.float32) / span
    )
    rows = positions.astype(jnp.float32)
    shape = (n, HEAD_DIM)
    columns = [jnp.broadcast_to(as_column(rows[i : i + 1]), shape) for i in range(3)]
    chosen = jnp.where(first, columns[0], jnp.where(second, columns[1], columns[2]))
    angles = chosen * frequency
    sine = jnp.sin(angles)
    odd = (channel % 2) == 1
    return jnp.cos(angles), jnp.where(odd, sine, -sine)


def swap_matrix(size):
    row = lax.broadcasted_iota(jnp.int32, (size, size), 0)
    column = lax.broadcasted_iota(jnp.int32, (size, size), 1)
    return jnp.where((row ^ 1) == column, 1.0, 0.0).astype(jnp.bfloat16)


def swapped_gain(gain):
    rows = jnp.broadcast_to(gain, (8, HEAD_DIM))
    odd = (lax.broadcasted_iota(jnp.int32, rows.shape, 1) % 2) == 1
    down = pltpu.roll(rows, 1, axis=1)
    up = pltpu.roll(rows, HEAD_DIM - 1, axis=1)
    return jnp.where(odd, down, up)[0:1]


def norm_factor(values):
    return lax.rsqrt(jnp.mean(values * values, axis=-1, keepdims=True) + eps)


def pack_kernel(group_rows, *refs):
    sources, out_ref, code_ref, held = refs[:8], refs[8], refs[9], refs[10:18]
    sent_ref, pick_ref, sems, out_sems = refs[18:]
    copies = [
        pltpu.make_async_copy(source, target, sems.at[i])
        for i, (source, target) in enumerate(zip(sources, held))
    ]
    for i in (7, 6, 4, 5, 0, 1, 2, 3):
        copies[i].start()
    query_ref, key_ref, value_ref, grad_ref = held[:4]
    query_gain_ref, key_gain_ref, positions_ref, place_ref = held[4:]
    slots, n = pick_ref.shape
    grp_count = out_ref.shape[0]
    narrow = query_ref.shape[1] // grp_count

    copies[7].wait()
    place = place_ref[...]
    slot = slot_of_token(place, group_rows).astype(jnp.int32)
    pick = lax.broadcasted_iota(jnp.int32, (slots, n), 0) == jnp.broadcast_to(slot, (slots, n))
    pick_ref[...] = jnp.where(pick, 1.0, 0.0).astype(jnp.bfloat16)
    rank = lax.broadcasted_iota(jnp.int32, (CAP, n), 0) == (slot & (CAP - 1))
    code = jnp.where(rank, ((place & (n - 1)) + 1).astype(jnp.float32), 0.0).astype(jnp.bfloat16)
    target = lax.broadcasted_iota(jnp.int32, (n, n), 0) == (slot // CAP)
    target = jnp.where(target, 1.0, 0.0).astype(jnp.bfloat16)
    code_ref[...] = f32_dot(code, target, ((1,), (1,))).astype(jnp.bfloat16)
    copies[6].wait()
    cosine, sine = rotation(positions_ref[...])
    swap = swap_matrix(narrow)
    copies[4].wait()
    copies[5].wait()
    turns = [
        (gain_ref[...] * cosine, swapped_gain(gain_ref[...]) * sine)
        for gain_ref in (query_gain_ref, key_gain_ref)
    ]
    for i in (0, 1, 2, 3):
        copies[i].wait()

    sends = []
    for h in range(grp_count):
        block = slice(h * narrow, (h + 1) * narrow)
        parts = []
        for ref, (along, across) in zip((query_ref, key_ref), turns):
            rows = ref[:, block]
            other = f32_dot(rows, swap, ((1,), (0,)))
            for start in range(0, narrow, HEAD_DIM):
                lanes = slice(start, start + HEAD_DIM)
                values = rows[:, lanes].astype(jnp.float32)
                rotated = (values * along + other[:, lanes] * across) * norm_factor(values)
                parts.append(rotated.astype(jnp.bfloat16))
        rows = jnp.concatenate(parts + [value_ref[:, block], grad_ref[:, block]], axis=1)
        sent_ref[h] = f32_dot(pick_ref[...], rows, ((1,), (0,))).astype(jnp.bfloat16)
        sends.append(pltpu.make_async_copy(sent_ref.at[h], out_ref.at[h], out_sems.at[h]))
        sends[-1].start()
    for send in sends:
        send.wait()


def attend_kernel(
    arrived_ref,
    near_ref,
    mine_ref,
    theirs_ref,
    spot_ref,
    clip_ref,
    out_ref,
    code_ref,
    token_ref,
    pick_ref,
    query_clip_ref,
    key_clip_ref,
    weights_ref,
    scores_ref,
    by_query_ref,
    by_key_ref,
):
    grp_count, slots, _ = arrived_ref.shape
    rows, columns = token_ref.shape
    width = columns // 4
    own = rows // grp_count
    block = rows // 4
    bf16 = jnp.bfloat16

    here, core = spot_ref[0], spot_ref[1]
    half = Z_COUNT // 2
    here_y, here_z = here // Z_COUNT, here & (Z_COUNT - 1)

    def put_codes(ref, entry, back_z, back_y):
        source_y = (here_y - back_y) & (Y_COUNT - 1)
        source_z = (here_z - back_z) & (Z_COUNT - 1)
        start = pl.multiple_of((source_y * Z_COUNT + source_z) * CAP, CAP)
        code_ref[pl.ds(start, CAP), :] = ref[entry].astype(jnp.float32)

    for back_y in range(Y_COUNT):
        put_codes(near_ref, back_y, 0, back_y)
        for step in range(1, half + 1):
            entry = (step - 1) * Y_COUNT + back_y
            put_codes(mine_ref, entry, step + (half - 1) * core, back_y)
            put_codes(theirs_ref, entry, step + (half - 1) * (1 - core), back_y)

    dp_count = slots // CAP
    codes = code_ref[...].astype(bf16)
    lane = lax.broadcasted_iota(jnp.int32, (rows, slots), 1)
    grp = lax.broadcasted_iota(jnp.int32, (rows, slots), 0) // own
    chosen = jnp.where(lane == grp * dp_count + here, 1.0, 0.0).astype(bf16)
    by_slot = f32_dot(codes, chosen, ((1,), (1,)))
    by_place = f32_dot(chosen, codes, ((1,), (1,)))
    across = (lax.broadcasted_iota(jnp.int32, (slots, own), 1) + 1).astype(jnp.float32)
    down = (lax.broadcasted_iota(jnp.int32, (own, slots), 0) + 1).astype(jnp.float32)

    for g in range(grp_count):
        part = slice(g * own, (g + 1) * own)
        pick_ref[g] = jnp.where(by_slot[:, part] == across, 1.0, 0.0).astype(bf16)
        pick = jnp.where(by_place[part] == down, 1.0, 0.0).astype(bf16)
        token_ref[part, :] = f32_dot(pick, arrived_ref[g], ((1,), (0,))).astype(bf16)

    first_rows = jnp.sum((clip_ref[...] == 0).astype(jnp.float32), axis=1, keepdims=True)
    place = lax.broadcasted_iota(jnp.int32, (rows, HEAD_DIM), 0).astype(jnp.float32)
    channel = lax.broadcasted_iota(jnp.int32, (rows, HEAD_DIM), 1)
    clip = jnp.where(place >= first_rows, 1, 0)
    query_clip_ref[...] = jnp.where(channel == clip, 1.0, 0.0).astype(bf16)
    key_clip_ref[...] = jnp.where(channel == 1 - clip, -4096.0, 0.0).astype(bf16)

    spans = [(0, 3 * block), (0, rows), (0, rows), (block, rows)]
    for head in range(width // HEAD_DIM):
        at = [slice(a * width + head * HEAD_DIM, a * width + (head + 1) * HEAD_DIM) for a in range(4)]
        for i, (low, high) in enumerate(spans):
            part = slice(i * block, (i + 1) * block)
            query = token_ref[part, at[0]]
            key = token_ref[low:high, at[1]]
            value = token_ref[low:high, at[2]]
            grad = token_ref[part, at[3]]
            scores = f32_dot(
                jnp.concatenate([query, query_clip_ref[part, :]], axis=1),
                jnp.concatenate([key, key_clip_ref[low:high, :]], axis=1),
                ((1,), (1,)),
            )
            raised = jnp.exp2(scores * (factor * math.log2(math.e)))
            weights = raised * (1.0 / jnp.sum(raised, axis=1, keepdims=True))
            weights_low = weights.astype(bf16)
            weights_ref[part, low:high] = weights_low
            attended = f32_dot(weights_low, value, ((1,), (0,))).astype(bf16)
            by_query_ref[part, head * HEAD_DIM : (head + 1) * HEAD_DIM] = attended
            row_dot = jnp.sum(
                grad.astype(jnp.float32) * attended.astype(jnp.float32), axis=1, keepdims=True
            )
            grad_weights = f32_dot(grad, value, ((1,), (1,)))
            grad_scores = (weights * (grad_weights - row_dot)).astype(bf16)
            scores_ref[part, low:high] = grad_scores
            grad_query = f32_dot(grad_scores, key, ((1,), (0,))) * factor
            by_query_ref[part, width + head * HEAD_DIM : width + (head + 1) * HEAD_DIM] = (
                grad_query.astype(bf16)
            )
        meets = [(0, block, 0, 3 * block), (block, 3 * block, 0, rows), (3 * block, rows, block, rows)]
        for low, high, first, last in meets:
            query = token_ref[first:last, at[0]]
            grad = token_ref[first:last, at[3]]
            channels = slice(head * HEAD_DIM, (head + 1) * HEAD_DIM)
            by_key_ref[0, channels, low:high] = (
                f32_dot(query, scores_ref[first:last, low:high], ((0,), (0,))) * factor
            ).astype(bf16)
            by_key_ref[1, channels, low:high] = f32_dot(
                grad, weights_ref[first:last, low:high], ((0,), (0,))
            ).astype(bf16)

    for g in range(grp_count):
        pick = pick_ref[g]
        part = slice(g * own, (g + 1) * own)
        out_ref[g, :, : 2 * width] = f32_dot(pick, by_query_ref[part, :], ((1,), (0,))).astype(bf16)
        for index in range(2):
            out_ref[g, :, (2 + index) * width : (3 + index) * width] = f32_dot(
                pick, by_key_ref[index, :, part], ((1,), (1,))
            ).astype(bf16)


def unpack_kernel(
    group_rows,
    back_ref,
    query_ref,
    key_ref,
    query_gain_ref,
    key_gain_ref,
    positions_ref,
    place_ref,
    *refs,
):
    outs, held, sems = refs[:4], refs[4:8], refs[8]
    grp_count, slots, _ = back_ref.shape
    n, width = query_ref.shape
    narrow = width // grp_count
    copies = [
        pltpu.make_async_copy(source, target, sems.at[i])
        for i, (source, target) in enumerate(zip(held, outs))
    ]
    slot = as_column(slot_of_token(place_ref[...], group_rows)).astype(jnp.int32)
    pick = jnp.broadcast_to(slot, (n, slots)) == lax.broadcasted_iota(jnp.int32, (n, slots), 1)
    pick = jnp.where(pick, 1.0, 0.0).astype(jnp.bfloat16)

    def take(h, index):
        rows = back_ref[h, :, index * narrow : (index + 1) * narrow]
        return f32_dot(pick, rows, ((1,), (0,)))

    for index, out in ((0, 0), (3, 3)):
        for h in range(grp_count):
            held[out][:, h * narrow : (h + 1) * narrow] = take(h, index).astype(jnp.bfloat16)
        copies[out].start()

    cosine, sine = rotation(positions_ref[...])
    swap = swap_matrix(narrow)
    for index, ref, gain_ref in ((1, query_ref, query_gain_ref), (2, key_ref, key_gain_ref)):
        along = cosine * gain_ref[...]
        across = sine * gain_ref[...]
        for h in range(grp_count):
            grads = take(h, index)
            other = f32_dot(grads.astype(jnp.bfloat16), swap, ((1,), (0,)))
            for start in range(0, narrow, HEAD_DIM):
                lanes = slice(h * narrow + start, h * narrow + start + HEAD_DIM)
                inner = slice(start, start + HEAD_DIM)
                values = ref[:, lanes].astype(jnp.float32)
                scale = norm_factor(values)
                grad = grads[:, inner] * along - other[:, inner] * across
                unit = values * scale
                share = jnp.mean(grad * unit, axis=-1, keepdims=True)
                held[index][:, lanes] = (scale * (grad - unit * share)).astype(jnp.bfloat16)
        copies[index].start()
    for copy in copies:
        copy.wait()


def gather_codes(codes):
    grp_count = lax.axis_size("grp")
    here = lax.all_gather(codes, "grp", axis=0)
    here = jnp.transpose(here, (1, 0, 2)).reshape(1, codes.shape[0], -1)
    spots = [(y, z) for y in range(Y_COUNT) for z in range(Z_COUNT)]

    def y_step(step):
        pairs = [(y * Z_COUNT + z, (y + step) % Y_COUNT * Z_COUNT + z) for y, z in spots]
        return lax.ppermute(here, "dp", pairs)

    near = jnp.concatenate([here] + [y_step(step) for step in range(1, Y_COUNT)], axis=0)
    half = Z_COUNT // 2

    def z_step(step):
        pairs = []
        for y, z in spots:
            for grp in range(grp_count):
                target = (z + step + (half - 1) * (grp % 2)) % Z_COUNT
                pairs.append(
                    ((y * Z_COUNT + z) * grp_count + grp, (y * Z_COUNT + target) * grp_count + grp)
                )
        return lax.ppermute(near, ("dp", "grp"), pairs)

    mine = jnp.concatenate([z_step(step) for step in range(1, half + 1)], axis=0)
    theirs = lax.ppermute(mine, "grp", [(grp, grp ^ 1) for grp in range(grp_count)])
    return near, mine, theirs


def on_device(
    query_in, key_in, value_in, out_grad, query_gain, key_gain, positions, token_place, clip_index
):
    n, width = query_in.shape
    dp_count = lax.axis_size("dp")
    grp_count = lax.axis_size("grp")
    group_rows = n * grp_count
    slots = dp_count * CAP
    narrow = width // grp_count
    query_gain = query_gain.reshape(1, HEAD_DIM)
    key_gain = key_gain.reshape(1, HEAD_DIM)
    place = token_place.reshape(1, n)
    bf16 = jnp.bfloat16
    vmem = pltpu.VMEM
    arguments = (query_in, key_in, value_in, out_grad, query_gain, key_gain, positions, place)
    in_hbm = pl.BlockSpec(memory_space=pltpu.HBM)
    sent_shape = (grp_count, slots, 4 * narrow)

    packed, codes = pl.pallas_call(
        functools.partial(pack_kernel, group_rows),
        name="pack",
        in_specs=[in_hbm] * 8,
        out_specs=[in_hbm, pl.BlockSpec(memory_space=pltpu.VMEM)],
        out_shape=[
            jax.ShapeDtypeStruct(sent_shape, bf16),
            jax.ShapeDtypeStruct((CAP, n), bf16),
        ],
        scratch_shapes=[vmem(a.shape, a.dtype) for a in arguments]
        + [
            vmem(sent_shape, bf16),
            vmem((slots, n), bf16),
            pltpu.SemaphoreType.DMA((8,)),
            pltpu.SemaphoreType.DMA((grp_count,)),
        ],
        compiler_params=pltpu.CompilerParams(vmem_limit_bytes=60 * MB),
    )(*arguments)

    def exchange(array):
        flat = array.reshape(dp_count * grp_count, CAP, array.shape[2])
        moved = lax.all_to_all(flat, ("grp", "dp"), split_axis=0, concat_axis=0, tiled=True)
        return moved.reshape(array.shape)

    arrived = exchange(packed)
    near, mine, theirs = gather_codes(codes[:, :dp_count])
    spot = jnp.stack([lax.axis_index("dp"), lax.axis_index("grp") % 2]).astype(jnp.int32)
    results = pl.pallas_call(
        attend_kernel,
        name="attend",
        in_specs=[pl.BlockSpec(memory_space=pltpu.VMEM)] * 4
        + [pl.BlockSpec(memory_space=pltpu.SMEM), pl.BlockSpec(memory_space=pltpu.VMEM)],
        out_shape=jax.ShapeDtypeStruct((grp_count, slots, 4 * narrow), bf16),
        scratch_shapes=[
            vmem((slots, slots), jnp.float32),
            vmem((group_rows, 4 * narrow), bf16),
            vmem((grp_count, slots, n), bf16),
            vmem((group_rows, HEAD_DIM), bf16),
            vmem((group_rows, HEAD_DIM), bf16),
            vmem((group_rows, group_rows), bf16),
            vmem((group_rows, group_rows), bf16),
            vmem((group_rows, 2 * narrow), bf16),
            vmem((2, narrow, group_rows), bf16),
        ],
        compiler_params=pltpu.CompilerParams(vmem_limit_bytes=40 * MB),
    )(arrived, near, mine, theirs, spot, clip_index)
    back = exchange(results)

    small = (query_gain, key_gain, positions, place)
    return pl.pallas_call(
        functools.partial(unpack_kernel, group_rows),
        name="unpack",
        out_specs=[in_hbm] * 4,
        out_shape=[jax.ShapeDtypeStruct((n, width), bf16)] * 4,
        scratch_shapes=[vmem((n, width), bf16)] * 4 + [pltpu.SemaphoreType.DMA((4,))],
        compiler_params=pltpu.CompilerParams(vmem_limit_bytes=24 * MB),
    )(back, query_in, key_in, *small)


def solution(mesh):
    rows = P(("dp", "grp"), None)
    in_specs = (
        rows,
        rows,
        rows,
        rows,
        P(),
        P(),
        P(None, ("dp", "grp")),
        P(("dp", "grp")),
        P("dp", None),
    )

    def run(*arrays):
        return tuple(on_device(*arrays))

    return jax.shard_map(
        run, mesh=mesh, in_specs=in_specs, out_specs=(rows,) * 4, check_vma=False
    )
```

```python
import functools
import math

import jax
import jax.numpy as jnp
from jax import lax
from jax.experimental import pallas as pl
from jax.experimental.pallas import tpu as pltpu
from jax.sharding import PartitionSpec as P

HEAD_DIM = 128
ROPE_T = 16
CAP = 8
Y_COUNT = 4
Z_COUNT = 8
eps = 1e-06
rope_base = 256.0
factor = 1.0 / math.sqrt(HEAD_DIM)
MB = 1024 * 1024


def f32_dot(a, b, dims):
    return lax.dot_general(a, b, (dims, ((), ())), preferred_element_type=jnp.float32)


def as_column(row):
    n = row.shape[1]
    eye = lax.broadcasted_iota(jnp.int32, (n, n), 0) == lax.broadcasted_iota(jnp.int32, (n, n), 1)
    return jnp.sum(jnp.where(eye, jnp.broadcast_to(row, (n, n)), 0.0), axis=1, keepdims=True)


def slot_of_token(place_row, group_rows):
    n = place_row.shape[1]
    target = (place_row // group_rows).astype(jnp.float32)
    column = as_column(target)
    earlier = lax.broadcasted_iota(jnp.int32, (n, n), 0) < lax.broadcasted_iota(
        jnp.int32, (n, n), 1
    )
    same = (column == jnp.broadcast_to(target, (n, n))) & earlier
    rank = jnp.sum(jnp.where(same, 1.0, 0.0), axis=0, keepdims=True)
    return target * CAP + rank


def rotation(positions):
    n = positions.shape[1]
    channel = lax.broadcasted_iota(jnp.int32, (1, HEAD_DIM), 1)
    pair = channel // 2
    time_pairs = ROPE_T // 2
    space_pairs = (HEAD_DIM - ROPE_T) // 4
    first = pair < time_pairs
    second = pair < time_pairs + space_pairs
    offset = jnp.where(first, 0, jnp.where(second, time_pairs, time_pairs + space_pairs))
    span = jnp.where(first, float(ROPE_T), float((HEAD_DIM - ROPE_T) // 2))
    frequency = jnp.exp(
        (-2.0 * math.log(rope_base)) * (pair - offset).astype(jnp.float32) / span
    )
    rows = positions.astype(jnp.float32)
    shape = (n, HEAD_DIM)
    columns = [jnp.broadcast_to(as_column(rows[i : i + 1]), shape) for i in range(3)]
    chosen = jnp.where(first, columns[0], jnp.where(second, columns[1], columns[2]))
    angles = chosen * frequency
    sine = jnp.sin(angles)
    odd = (channel % 2) == 1
    return jnp.cos(angles), jnp.where(odd, sine, -sine)


def swap_matrix(size):
    row = lax.broadcasted_iota(jnp.int32, (size, size), 0)
    column = lax.broadcasted_iota(jnp.int32, (size, size), 1)
    return jnp.where((row ^ 1) == column, 1.0, 0.0).astype(jnp.bfloat16)


def swapped_gain(gain):
    rows = jnp.broadcast_to(gain, (8, HEAD_DIM))
    odd = (lax.broadcasted_iota(jnp.int32, rows.shape, 1) % 2) == 1
    down = pltpu.roll(rows, 1, axis=1)
    up = pltpu.roll(rows, HEAD_DIM - 1, axis=1)
    return jnp.where(odd, down, up)[0:1]


def norm_factor(values):
    return lax.rsqrt(jnp.mean(values * values, axis=-1, keepdims=True) + eps)


def pack_kernel(group_rows, *refs):
    sources, out_ref, code_ref, held = refs[:8], refs[8], refs[9], refs[10:18]
    sent_ref, pick_ref, sems, out_sems = refs[18:]
    copies = [
        pltpu.make_async_copy(source, target, sems.at[i])
        for i, (source, target) in enumerate(zip(sources, held))
    ]
    for i in (7, 6, 4, 5, 0, 1, 2, 3):
        copies[i].start()
    query_ref, key_ref, value_ref, grad_ref = held[:4]
    query_gain_ref, key_gain_ref, positions_ref, place_ref = held[4:]
    slots, n = pick_ref.shape
    grp_count = out_ref.shape[0]
    narrow = query_ref.shape[1] // grp_count

    copies[7].wait()
    place = place_ref[...]
    slot = slot_of_token(place, group_rows).astype(jnp.int32)
    pick = lax.broadcasted_iota(jnp.int32, (slots, n), 0) == jnp.broadcast_to(slot, (slots, n))
    pick_ref[...] = jnp.where(pick, 1.0, 0.0).astype(jnp.bfloat16)
    rank = lax.broadcasted_iota(jnp.int32, (CAP, n), 0) == (slot & (CAP - 1))
    code = jnp.where(rank, ((place & (n - 1)) + 1).astype(jnp.float32), 0.0).astype(jnp.bfloat16)
    target = lax.broadcasted_iota(jnp.int32, (n, n), 0) == (slot // CAP)
    target = jnp.where(target, 1.0, 0.0).astype(jnp.bfloat16)
    code_ref[...] = f32_dot(code, target, ((1,), (1,)))
    copies[6].wait()
    cosine, sine = rotation(positions_ref[...])
    swap = swap_matrix(narrow)
    copies[4].wait()
    copies[5].wait()
    turns = [
        (gain_ref[...] * cosine, swapped_gain(gain_ref[...]) * sine)
        for gain_ref in (query_gain_ref, key_gain_ref)
    ]
    for i in (0, 1, 2, 3):
        copies[i].wait()

    sends = []
    for h in range(grp_count):
        block = slice(h * narrow, (h + 1) * narrow)
        parts = []
        for ref, (along, across) in zip((query_ref, key_ref), turns):
            rows = ref[:, block]
            other = f32_dot(rows, swap, ((1,), (0,)))
            for start in range(0, narrow, HEAD_DIM):
                lanes = slice(start, start + HEAD_DIM)
                values = rows[:, lanes].astype(jnp.float32)
                rotated = (values * along + other[:, lanes] * across) * norm_factor(values)
                parts.append(rotated.astype(jnp.bfloat16))
        rows = jnp.concatenate(parts + [value_ref[:, block], grad_ref[:, block]], axis=1)
        sent_ref[h] = f32_dot(pick_ref[...], rows, ((1,), (0,))).astype(jnp.bfloat16)
        sends.append(pltpu.make_async_copy(sent_ref.at[h], out_ref.at[h], out_sems.at[h]))
        sends[-1].start()
    for send in sends:
        send.wait()


def attend_kernel(
    arrived_ref,
    near_ref,
    mine_ref,
    theirs_ref,
    spot_ref,
    clip_ref,
    out_ref,
    code_ref,
    token_ref,
    pick_ref,
    query_clip_ref,
    key_clip_ref,
    by_query_ref,
    by_key_ref,
):
    grp_count, slots, _ = arrived_ref.shape
    rows, columns = token_ref.shape
    width = columns // 4
    own = rows // grp_count
    bf16 = jnp.bfloat16

    here, core = spot_ref[0], spot_ref[1]
    half = Z_COUNT // 2
    here_y, here_z = here // Z_COUNT, here & (Z_COUNT - 1)

    steps = lax.broadcasted_iota(jnp.int32, (CAP, code_ref.shape[1]), 1) // grp_count

    def put_codes(codes, back_z):
        source_z = (here_z - back_z) & (Z_COUNT - 1)
        for back_y in range(Y_COUNT):
            source_y = (here_y - back_y) & (Y_COUNT - 1)
            start = pl.multiple_of((source_y * Z_COUNT + source_z) * CAP, CAP)
            code_ref[pl.ds(start, CAP), :] = jnp.where(steps == back_y, codes, 0.0)

    put_codes(near_ref[0], 0)
    for step in range(1, half + 1):
        put_codes(mine_ref[step - 1], step + (half - 1) * core)
        put_codes(theirs_ref[step - 1], step + (half - 1) * (1 - core))

    codes = code_ref[...].astype(bf16)
    shape = (rows, codes.shape[1])
    lane = lax.broadcasted_iota(jnp.int32, shape, 1) & (grp_count - 1)
    chosen = jnp.where(lane == lax.broadcasted_iota(jnp.int32, shape, 0) // own, 1.0, 0.0).astype(bf16)
    by_slot = f32_dot(codes, chosen, ((1,), (1,)))
    by_place = f32_dot(chosen, codes, ((1,), (1,)))
    across = (lax.broadcasted_iota(jnp.int32, (slots, own), 1) + 1).astype(jnp.float32)
    down = (lax.broadcasted_iota(jnp.int32, (own, slots), 0) + 1).astype(jnp.float32)

    for g in range(grp_count):
        part = slice(g * own, (g + 1) * own)
        pick_ref[g] = jnp.where(by_slot[:, part] == across, 1.0, 0.0).astype(bf16)
        pick = jnp.where(by_place[part] == down, 1.0, 0.0).astype(bf16)
        token_ref[part, :] = f32_dot(pick, arrived_ref[g], ((1,), (0,))).astype(bf16)

    first_rows = jnp.sum((clip_ref[...] == 0).astype(jnp.float32), axis=1, keepdims=True)
    place = lax.broadcasted_iota(jnp.int32, (rows, HEAD_DIM), 0).astype(jnp.float32)
    channel = lax.broadcasted_iota(jnp.int32, (rows, HEAD_DIM), 1)
    clip = jnp.where(place >= first_rows, 1, 0)
    query_clip_ref[...] = jnp.where(channel == clip, 1.0, 0.0).astype(bf16)
    key_clip_ref[...] = jnp.where(channel == 1 - clip, -4096.0, 0.0).astype(bf16)

    for head in range(width // HEAD_DIM):
        channels = slice(head * HEAD_DIM, (head + 1) * HEAD_DIM)
        query, key, value, grad = [
            token_ref[:, a * width + head * HEAD_DIM : a * width + (head + 1) * HEAD_DIM]
            for a in range(4)
        ]
        scores = f32_dot(
            jnp.concatenate([query, query_clip_ref[...]], axis=1),
            jnp.concatenate([key, key_clip_ref[...]], axis=1),
            ((1,), (1,)),
        )
        raised = jnp.exp2(scores * (factor * math.log2(math.e)))
        weights = raised * (1.0 / jnp.sum(raised, axis=1, keepdims=True))
        weights_low = weights.astype(bf16)
        attended = f32_dot(weights_low, value, ((1,), (0,))).astype(bf16)
        by_query_ref[:, channels] = attended
        row_dot = jnp.sum(
            grad.astype(jnp.float32) * attended.astype(jnp.float32), axis=1, keepdims=True
        )
        grad_weights = f32_dot(grad, value, ((1,), (1,)))
        grad_scores = (weights * (grad_weights - row_dot)).astype(bf16)
        grad_query = f32_dot(grad_scores, key, ((1,), (0,))) * factor
        by_query_ref[:, width + head * HEAD_DIM : width + (head + 1) * HEAD_DIM] = (
            grad_query.astype(bf16)
        )
        grad_key = f32_dot(query, grad_scores, ((0,), (0,))) * factor
        by_key_ref[0, channels, :] = grad_key.astype(bf16)
        by_key_ref[1, channels, :] = f32_dot(grad, weights_low, ((0,), (0,))).astype(bf16)

    for g in range(grp_count):
        pick = pick_ref[g]
        part = slice(g * own, (g + 1) * own)
        out_ref[g, :, : 2 * width] = f32_dot(pick, by_query_ref[part, :], ((1,), (0,))).astype(bf16)
        for index in range(2):
            out_ref[g, :, (2 + index) * width : (3 + index) * width] = f32_dot(
                pick, by_key_ref[index, :, part], ((1,), (1,))
            ).astype(bf16)


def unpack_kernel(
    group_rows,
    back_ref,
    query_ref,
    key_ref,
    query_gain_ref,
    key_gain_ref,
    positions_ref,
    place_ref,
    *refs,
):
    outs, held, sems = refs[:4], refs[4:8], refs[8]
    grp_count, slots, _ = back_ref.shape
    n, width = query_ref.shape
    narrow = width // grp_count
    copies = [
        pltpu.make_async_copy(source, target, sems.at[i])
        for i, (source, target) in enumerate(zip(held, outs))
    ]
    slot = as_column(slot_of_token(place_ref[...], group_rows)).astype(jnp.int32)
    pick = jnp.broadcast_to(slot, (n, slots)) == lax.broadcasted_iota(jnp.int32, (n, slots), 1)
    pick = jnp.where(pick, 1.0, 0.0).astype(jnp.bfloat16)

    def take(h, index):
        rows = back_ref[h, :, index * narrow : (index + 1) * narrow]
        return f32_dot(pick, rows, ((1,), (0,)))

    for index, out in ((0, 0), (3, 3)):
        for h in range(grp_count):
            held[out][:, h * narrow : (h + 1) * narrow] = take(h, index).astype(jnp.bfloat16)
        copies[out].start()

    cosine, sine = rotation(positions_ref[...])
    swap = swap_matrix(narrow)
    for index, ref, gain_ref in ((1, query_ref, query_gain_ref), (2, key_ref, key_gain_ref)):
        along = cosine * gain_ref[...]
        across = sine * gain_ref[...]
        for h in range(grp_count):
            grads = take(h, index)
            other = f32_dot(grads.astype(jnp.bfloat16), swap, ((1,), (0,)))
            for start in range(0, narrow, HEAD_DIM):
                lanes = slice(h * narrow + start, h * narrow + start + HEAD_DIM)
                inner = slice(start, start + HEAD_DIM)
                values = ref[:, lanes].astype(jnp.float32)
                scale = norm_factor(values)
                grad = grads[:, inner] * along - other[:, inner] * across
                unit = values * scale
                share = jnp.mean(grad * unit, axis=-1, keepdims=True)
                held[index][:, lanes] = (scale * (grad - unit * share)).astype(jnp.bfloat16)
        copies[index].start()
    for copy in copies:
        copy.wait()


def gather_codes(codes):
    grp_count = lax.axis_size("grp")
    dp_index = lax.axis_index("dp")
    core = lax.axis_index("grp") % 2
    here = lax.all_gather(codes, "grp", axis=0)
    spots = [(y, z) for y in range(Y_COUNT) for z in range(Z_COUNT)]

    def y_step(step):
        pairs = [(y * Z_COUNT + z, (y + step) % Y_COUNT * Z_COUNT + z) for y, z in spots]
        return lax.ppermute(here, "dp", pairs)

    along_y = jnp.stack([here] + [y_step(step) for step in range(1, Y_COUNT)])
    along_y = along_y.reshape(Y_COUNT, grp_count, CAP, Y_COUNT, Z_COUNT)
    along_y = lax.dynamic_index_in_dim(along_y, dp_index // Z_COUNT, axis=3, keepdims=False)
    by_target = jnp.transpose(along_y, (3, 2, 0, 1)).reshape(Z_COUNT, CAP, Y_COUNT * grp_count)
    half = Z_COUNT // 2

    def for_step(step):
        target = (dp_index + step) % Z_COUNT
        return lax.dynamic_slice_in_dim(by_target, target, 1, axis=0)

    def z_step(step):
        pairs = []
        for y, z in spots:
            for grp in range(grp_count):
                target = (z + step + (half - 1) * (grp % 2)) % Z_COUNT
                pairs.append(
                    ((y * Z_COUNT + z) * grp_count + grp, (y * Z_COUNT + target) * grp_count + grp)
                )
        return lax.ppermute(for_step(step + (half - 1) * core), ("dp", "grp"), pairs)

    mine = jnp.concatenate([z_step(step) for step in range(1, half + 1)], axis=0)
    theirs = lax.ppermute(mine, "grp", [(grp, grp ^ 1) for grp in range(grp_count)])
    return for_step(0), mine, theirs


def on_device(
    query_in, key_in, value_in, out_grad, query_gain, key_gain, positions, token_place, clip_index
):
    n, width = query_in.shape
    dp_count = lax.axis_size("dp")
    grp_count = lax.axis_size("grp")
    group_rows = n * grp_count
    slots = dp_count * CAP
    narrow = width // grp_count
    query_gain = query_gain.reshape(1, HEAD_DIM)
    key_gain = key_gain.reshape(1, HEAD_DIM)
    place = token_place.reshape(1, n)
    bf16 = jnp.bfloat16
    vmem = pltpu.VMEM
    arguments = (query_in, key_in, value_in, out_grad, query_gain, key_gain, positions, place)
    in_hbm = pl.BlockSpec(memory_space=pltpu.HBM)
    sent_shape = (grp_count, slots, 4 * narrow)

    packed, codes = pl.pallas_call(
        functools.partial(pack_kernel, group_rows),
        name="pack",
        in_specs=[in_hbm] * 8,
        out_specs=[in_hbm, pl.BlockSpec(memory_space=pltpu.VMEM)],
        out_shape=[
            jax.ShapeDtypeStruct(sent_shape, bf16),
            jax.ShapeDtypeStruct((CAP, n), jnp.float32),
        ],
        scratch_shapes=[vmem(a.shape, a.dtype) for a in arguments]
        + [
            vmem(sent_shape, bf16),
            vmem((slots, n), bf16),
            pltpu.SemaphoreType.DMA((8,)),
            pltpu.SemaphoreType.DMA((grp_count,)),
        ],
        compiler_params=pltpu.CompilerParams(vmem_limit_bytes=60 * MB),
    )(*arguments)

    def exchange(array):
        flat = array.reshape(dp_count * grp_count, CAP, array.shape[2])
        moved = lax.all_to_all(flat, ("grp", "dp"), split_axis=0, concat_axis=0, tiled=True)
        return moved.reshape(array.shape)

    arrived = exchange(packed)
    near, mine, theirs = gather_codes(codes[:, :dp_count])
    spot = jnp.stack([lax.axis_index("dp"), lax.axis_index("grp") % 2]).astype(jnp.int32)
    results = pl.pallas_call(
        attend_kernel,
        name="attend",
        in_specs=[pl.BlockSpec(memory_space=pltpu.VMEM)] * 4
        + [pl.BlockSpec(memory_space=pltpu.SMEM), pl.BlockSpec(memory_space=pltpu.VMEM)],
        out_shape=jax.ShapeDtypeStruct((grp_count, slots, 4 * narrow), bf16),
        scratch_shapes=[
            vmem((slots, near.shape[2]), jnp.float32),
            vmem((group_rows, 4 * narrow), bf16),
            vmem((grp_count, slots, n), bf16),
            vmem((group_rows, HEAD_DIM), bf16),
            vmem((group_rows, HEAD_DIM), bf16),
            vmem((group_rows, 2 * narrow), bf16),
            vmem((2, narrow, group_rows), bf16),
        ],
        compiler_params=pltpu.CompilerParams(vmem_limit_bytes=40 * MB),
    )(arrived, near, mine, theirs, spot, clip_index)
    back = exchange(results)

    small = (query_gain, key_gain, positions, place)
    return pl.pallas_call(
        functools.partial(unpack_kernel, group_rows),
        name="unpack",
        out_specs=[in_hbm] * 4,
        out_shape=[jax.ShapeDtypeStruct((n, width), bf16)] * 4,
        scratch_shapes=[vmem((n, width), bf16)] * 4 + [pltpu.SemaphoreType.DMA((4,))],
        compiler_params=pltpu.CompilerParams(vmem_limit_bytes=24 * MB),
    )(back, query_in, key_in, *small)


def solution(mesh):
    rows = P(("dp", "grp"), None)
    in_specs = (
        rows,
        rows,
        rows,
        rows,
        P(),
        P(),
        P(None, ("dp", "grp")),
        P(("dp", "grp")),
        P("dp", None),
    )

    def run(*arrays):
        return tuple(on_device(*arrays))

    return jax.shard_map(
        run, mesh=mesh, in_specs=in_specs, out_specs=(rows,) * 4, check_vma=False
    )
```

```python
import functools
import math

import jax
import jax.numpy as jnp
from jax import lax
from jax.experimental import pallas as pl
from jax.experimental.pallas import tpu as pltpu
from jax.sharding import PartitionSpec as P

HEAD_DIM = 128
ROPE_T = 16
CAP = 8
Y_COUNT = 4
Z_COUNT = 8
eps = 1e-06
rope_base = 256.0
factor = 1.0 / math.sqrt(HEAD_DIM)
MB = 1024 * 1024


def f32_dot(a, b, dims):
    return lax.dot_general(a, b, (dims, ((), ())), preferred_element_type=jnp.float32)


def as_column(row):
    n = row.shape[1]
    eye = lax.broadcasted_iota(jnp.int32, (n, n), 0) == lax.broadcasted_iota(jnp.int32, (n, n), 1)
    return jnp.sum(jnp.where(eye, jnp.broadcast_to(row, (n, n)), 0.0), axis=1, keepdims=True)


def slot_of_token(place_row, group_rows):
    n = place_row.shape[1]
    target = (place_row // group_rows).astype(jnp.float32)
    column = as_column(target)
    earlier = lax.broadcasted_iota(jnp.int32, (n, n), 0) < lax.broadcasted_iota(
        jnp.int32, (n, n), 1
    )
    same = (column == jnp.broadcast_to(target, (n, n))) & earlier
    rank = jnp.sum(jnp.where(same, 1.0, 0.0), axis=0, keepdims=True)
    return target * CAP + rank


def rotation(positions):
    n = positions.shape[1]
    channel = lax.broadcasted_iota(jnp.int32, (1, HEAD_DIM), 1)
    pair = channel // 2
    time_pairs = ROPE_T // 2
    space_pairs = (HEAD_DIM - ROPE_T) // 4
    first = pair < time_pairs
    second = pair < time_pairs + space_pairs
    offset = jnp.where(first, 0, jnp.where(second, time_pairs, time_pairs + space_pairs))
    span = jnp.where(first, float(ROPE_T), float((HEAD_DIM - ROPE_T) // 2))
    frequency = jnp.exp(
        (-2.0 * math.log(rope_base)) * (pair - offset).astype(jnp.float32) / span
    )
    rows = positions.astype(jnp.float32)
    shape = (n, HEAD_DIM)
    columns = [jnp.broadcast_to(as_column(rows[i : i + 1]), shape) for i in range(3)]
    chosen = jnp.where(first, columns[0], jnp.where(second, columns[1], columns[2]))
    angles = chosen * frequency
    sine = jnp.sin(angles)
    odd = (channel % 2) == 1
    return jnp.cos(angles), jnp.where(odd, sine, -sine)


def swap_matrix(size):
    row = lax.broadcasted_iota(jnp.int32, (size, size), 0)
    column = lax.broadcasted_iota(jnp.int32, (size, size), 1)
    return jnp.where((row ^ 1) == column, 1.0, 0.0).astype(jnp.bfloat16)


def swapped_gain(gain):
    rows = jnp.broadcast_to(gain, (8, HEAD_DIM))
    odd = (lax.broadcasted_iota(jnp.int32, rows.shape, 1) % 2) == 1
    down = pltpu.roll(rows, 1, axis=1)
    up = pltpu.roll(rows, HEAD_DIM - 1, axis=1)
    return jnp.where(odd, down, up)[0:1]


def norm_factor(values):
    return lax.rsqrt(jnp.mean(values * values, axis=-1, keepdims=True) + eps)


def pack_kernel(group_rows, *refs):
    sources, out_ref, code_ref, held = refs[:8], refs[8], refs[9], refs[10:18]
    sent_ref, pick_ref, sems, out_sems = refs[18:]
    copies = [
        pltpu.make_async_copy(source, target, sems.at[i])
        for i, (source, target) in enumerate(zip(sources, held))
    ]
    for i in (7, 6, 4, 5, 0, 1, 2, 3):
        copies[i].start()
    query_ref, key_ref, value_ref, grad_ref = held[:4]
    query_gain_ref, key_gain_ref, positions_ref, place_ref = held[4:]
    slots, n = pick_ref.shape
    grp_count = out_ref.shape[0]
    narrow = query_ref.shape[1] // grp_count

    copies[7].wait()
    place = place_ref[...]
    slot = slot_of_token(place, group_rows).astype(jnp.int32)
    pick = lax.broadcasted_iota(jnp.int32, (slots, n), 0) == jnp.broadcast_to(slot, (slots, n))
    pick_ref[...] = jnp.where(pick, 1.0, 0.0).astype(jnp.bfloat16)
    rank = lax.broadcasted_iota(jnp.int32, (CAP, n), 0) == (slot & (CAP - 1))
    code = jnp.where(rank, ((place & (n - 1)) + 1).astype(jnp.float32), 0.0).astype(jnp.bfloat16)
    target = lax.broadcasted_iota(jnp.int32, (n, n), 0) == (slot // CAP)
    target = jnp.where(target, 1.0, 0.0).astype(jnp.bfloat16)
    code_ref[...] = f32_dot(code, target, ((1,), (1,)))
    copies[6].wait()
    cosine, sine = rotation(positions_ref[...])
    swap = swap_matrix(narrow)
    copies[4].wait()
    copies[5].wait()
    turns = [
        (gain_ref[...] * cosine, swapped_gain(gain_ref[...]) * sine)
        for gain_ref in (query_gain_ref, key_gain_ref)
    ]
    for i in (0, 1, 2, 3):
        copies[i].wait()

    sends = []
    for h in range(grp_count):
        block = slice(h * narrow, (h + 1) * narrow)
        prepared = []
        for ref, (along, across) in zip((query_ref, key_ref), turns):
            rows = ref[:, block]
            other = f32_dot(rows, swap, ((1,), (0,)))
            for start in range(0, narrow, HEAD_DIM):
                lanes = slice(start, start + HEAD_DIM)
                values = rows[:, lanes].astype(jnp.float32)
                rotated = (values * along + other[:, lanes] * across) * norm_factor(values)
                prepared.append(rotated.astype(jnp.bfloat16))
        parts = []
        for head, start in enumerate(range(h * narrow, (h + 1) * narrow, HEAD_DIM)):
            lanes = slice(start, start + HEAD_DIM)
            parts += prepared[head :: narrow // HEAD_DIM] + [value_ref[:, lanes], grad_ref[:, lanes]]
        rows = jnp.concatenate(parts, axis=1)
        sent_ref[h] = f32_dot(pick_ref[...], rows, ((1,), (0,))).astype(jnp.bfloat16)
        sends.append(pltpu.make_async_copy(sent_ref.at[h], out_ref.at[h], out_sems.at[h]))
        sends[-1].start()
    for send in sends:
        send.wait()


def attend_kernel(
    arrived_ref,
    near_ref,
    mine_ref,
    theirs_ref,
    spot_ref,
    clip_ref,
    out_ref,
    slot_ref,
    code_ref,
    token_ref,
    pick_ref,
    order_ref,
    query_clip_ref,
    key_clip_ref,
    by_query_ref,
    by_key_ref,
    sems,
):
    grp_count, slots, _ = arrived_ref.shape
    rows, columns = token_ref.shape
    width = columns // 4
    share = 4 * HEAD_DIM
    heads = columns // share
    copies = []
    for head in range(heads):
        lanes = pl.ds(head * share, share)
        copies.append(
            pltpu.make_async_copy(
                arrived_ref.at[:, :, lanes], slot_ref.at[:, :, lanes], sems.at[head]
            )
        )
    copies[0].start()
    own = rows // grp_count
    bf16 = jnp.bfloat16

    here, core = spot_ref[0], spot_ref[1]
    half = Z_COUNT // 2
    here_y, here_z = here // Z_COUNT, here & (Z_COUNT - 1)

    steps = lax.broadcasted_iota(jnp.int32, (CAP, code_ref.shape[1]), 1) // grp_count

    def put_codes(codes, back_z):
        source_z = (here_z - back_z) & (Z_COUNT - 1)
        for back_y in range(Y_COUNT):
            source_y = (here_y - back_y) & (Y_COUNT - 1)
            start = pl.multiple_of((source_y * Z_COUNT + source_z) * CAP, CAP)
            code_ref[pl.ds(start, CAP), :] = jnp.where(steps == back_y, codes, 0.0)

    put_codes(near_ref[0], 0)
    for step in range(1, half + 1):
        put_codes(mine_ref[step - 1], step + (half - 1) * core)
        put_codes(theirs_ref[step - 1], step + (half - 1) * (1 - core))

    codes = code_ref[...].astype(bf16)
    shape = (rows, codes.shape[1])
    lane = lax.broadcasted_iota(jnp.int32, shape, 1) & (grp_count - 1)
    chosen = jnp.where(lane == lax.broadcasted_iota(jnp.int32, shape, 0) // own, 1.0, 0.0).astype(bf16)
    by_slot = f32_dot(codes, chosen, ((1,), (1,)))
    by_place = f32_dot(chosen, codes, ((1,), (1,)))
    across = (lax.broadcasted_iota(jnp.int32, (slots, own), 1) + 1).astype(jnp.float32)
    down = (lax.broadcasted_iota(jnp.int32, (own, slots), 0) + 1).astype(jnp.float32)

    for g in range(grp_count):
        part = slice(g * own, (g + 1) * own)
        pick_ref[g] = jnp.where(by_slot[:, part] == across, 1.0, 0.0).astype(bf16)
        order_ref[g] = jnp.where(by_place[part] == down, 1.0, 0.0).astype(bf16)

    first_rows = jnp.sum((clip_ref[...] == 0).astype(jnp.float32), axis=1, keepdims=True)
    place = lax.broadcasted_iota(jnp.int32, (rows, HEAD_DIM), 0).astype(jnp.float32)
    channel = lax.broadcasted_iota(jnp.int32, (rows, HEAD_DIM), 1)
    clip = jnp.where(place >= first_rows, 1, 0)
    query_clip_ref[...] = jnp.where(channel == clip, 1.0, 0.0).astype(bf16)
    key_clip_ref[...] = jnp.where(channel == 1 - clip, -4096.0, 0.0).astype(bf16)

    for head in range(heads):
        mine = slice(head * share, (head + 1) * share)
        copies[head].wait()
        if head + 1 < heads:
            copies[head + 1].start()
        for g in range(grp_count):
            token_ref[g * own : (g + 1) * own, mine] = f32_dot(
                order_ref[g], slot_ref[g, :, mine], ((1,), (0,))
            ).astype(bf16)
        channels = slice(head * HEAD_DIM, (head + 1) * HEAD_DIM)
        query, key, value, grad = [
            token_ref[:, head * share + a * HEAD_DIM : head * share + (a + 1) * HEAD_DIM]
            for a in range(4)
        ]
        scores = f32_dot(
            jnp.concatenate([query, query_clip_ref[...]], axis=1),
            jnp.concatenate([key, key_clip_ref[...]], axis=1),
            ((1,), (1,)),
        )
        raised = jnp.exp2(scores * (factor * math.log2(math.e)))
        weights = raised * (1.0 / jnp.sum(raised, axis=1, keepdims=True))
        weights_low = weights.astype(bf16)
        attended = f32_dot(weights_low, value, ((1,), (0,))).astype(bf16)
        by_query_ref[:, channels] = attended
        row_dot = jnp.sum(
            grad.astype(jnp.float32) * attended.astype(jnp.float32), axis=1, keepdims=True
        )
        grad_weights = f32_dot(grad, value, ((1,), (1,)))
        grad_scores = (weights * (grad_weights - row_dot)).astype(bf16)
        grad_query = f32_dot(grad_scores, key, ((1,), (0,))) * factor
        by_query_ref[:, width + head * HEAD_DIM : width + (head + 1) * HEAD_DIM] = (
            grad_query.astype(bf16)
        )
        grad_key = f32_dot(query, grad_scores, ((0,), (0,))) * factor
        by_key_ref[0, channels, :] = grad_key.astype(bf16)
        by_key_ref[1, channels, :] = f32_dot(grad, weights_low, ((0,), (0,))).astype(bf16)

    for g in range(grp_count):
        pick = pick_ref[g]
        part = slice(g * own, (g + 1) * own)
        out_ref[g, :, : 2 * width] = f32_dot(pick, by_query_ref[part, :], ((1,), (0,))).astype(bf16)
        for index in range(2):
            out_ref[g, :, (2 + index) * width : (3 + index) * width] = f32_dot(
                pick, by_key_ref[index, :, part], ((1,), (1,))
            ).astype(bf16)


def unpack_kernel(
    group_rows,
    back_ref,
    query_ref,
    key_ref,
    query_gain_ref,
    key_gain_ref,
    positions_ref,
    place_ref,
    *refs,
):
    outs, held, sems = refs[:4], refs[4:8], refs[8]
    grp_count, slots, _ = back_ref.shape
    n, width = query_ref.shape
    narrow = width // grp_count
    half = grp_count // 2

    def send(index, h):
        lanes = pl.ds((h // half) * half * narrow, half * narrow)
        return pltpu.make_async_copy(
            held[index].at[:, lanes], outs[index].at[:, lanes], sems.at[index, h // half]
        )

    slot = as_column(slot_of_token(place_ref[...], group_rows)).astype(jnp.int32)
    pick = jnp.broadcast_to(slot, (n, slots)) == lax.broadcasted_iota(jnp.int32, (n, slots), 1)
    pick = jnp.where(pick, 1.0, 0.0).astype(jnp.bfloat16)

    def take(h, index):
        rows = back_ref[h, :, index * narrow : (index + 1) * narrow]
        return f32_dot(pick, rows, ((1,), (0,)))

    for index, out in ((0, 0), (3, 3)):
        for h in range(grp_count):
            held[out][:, h * narrow : (h + 1) * narrow] = take(h, index).astype(jnp.bfloat16)
            if h % half == half - 1:
                send(out, h).start()

    cosine, sine = rotation(positions_ref[...])
    swap = swap_matrix(narrow)
    for index, ref, gain_ref in ((1, query_ref, query_gain_ref), (2, key_ref, key_gain_ref)):
        along = cosine * gain_ref[...]
        across = sine * gain_ref[...]
        for h in range(grp_count):
            grads = take(h, index)
            other = f32_dot(grads.astype(jnp.bfloat16), swap, ((1,), (0,)))
            for start in range(0, narrow, HEAD_DIM):
                lanes = slice(h * narrow + start, h * narrow + start + HEAD_DIM)
                inner = slice(start, start + HEAD_DIM)
                values = ref[:, lanes].astype(jnp.float32)
                scale = norm_factor(values)
                grad = grads[:, inner] * along - other[:, inner] * across
                unit = values * scale
                share = jnp.mean(grad * unit, axis=-1, keepdims=True)
                held[index][:, lanes] = (scale * (grad - unit * share)).astype(jnp.bfloat16)
            if h % half == half - 1:
                send(index, h).start()
    for index in range(4):
        for h in (0, half):
            send(index, h).wait()


def gather_codes(codes):
    grp_count = lax.axis_size("grp")
    dp_index = lax.axis_index("dp")
    core = lax.axis_index("grp") % 2
    here = lax.all_gather(codes, "grp", axis=0)
    spots = [(y, z) for y in range(Y_COUNT) for z in range(Z_COUNT)]

    def y_step(step):
        pairs = [(y * Z_COUNT + z, (y + step) % Y_COUNT * Z_COUNT + z) for y, z in spots]
        return lax.ppermute(here, "dp", pairs)

    along_y = jnp.stack([here] + [y_step(step) for step in range(1, Y_COUNT)])
    along_y = along_y.reshape(Y_COUNT, grp_count, CAP, Y_COUNT, Z_COUNT)
    along_y = lax.dynamic_index_in_dim(along_y, dp_index // Z_COUNT, axis=3, keepdims=False)
    by_target = jnp.transpose(along_y, (3, 2, 0, 1)).reshape(Z_COUNT, CAP, Y_COUNT * grp_count)
    half = Z_COUNT // 2

    def for_step(step):
        target = (dp_index + step) % Z_COUNT
        return lax.dynamic_slice_in_dim(by_target, target, 1, axis=0)

    def z_step(step):
        pairs = []
        for y, z in spots:
            for grp in range(grp_count):
                target = (z + step + (half - 1) * (grp % 2)) % Z_COUNT
                pairs.append(
                    ((y * Z_COUNT + z) * grp_count + grp, (y * Z_COUNT + target) * grp_count + grp)
                )
        return lax.ppermute(for_step(step + (half - 1) * core), ("dp", "grp"), pairs)

    mine = jnp.concatenate([z_step(step) for step in range(1, half + 1)], axis=0)
    theirs = lax.ppermute(mine, "grp", [(grp, grp ^ 1) for grp in range(grp_count)])
    return for_step(0), mine, theirs


def on_device(
    query_in, key_in, value_in, out_grad, query_gain, key_gain, positions, token_place, clip_index
):
    n, width = query_in.shape
    dp_count = lax.axis_size("dp")
    grp_count = lax.axis_size("grp")
    group_rows = n * grp_count
    slots = dp_count * CAP
    narrow = width // grp_count
    query_gain = query_gain.reshape(1, HEAD_DIM)
    key_gain = key_gain.reshape(1, HEAD_DIM)
    place = token_place.reshape(1, n)
    bf16 = jnp.bfloat16
    vmem = pltpu.VMEM
    arguments = (query_in, key_in, value_in, out_grad, query_gain, key_gain, positions, place)
    in_hbm = pl.BlockSpec(memory_space=pltpu.HBM)
    sent_shape = (grp_count, slots, 4 * narrow)

    packed, codes = pl.pallas_call(
        functools.partial(pack_kernel, group_rows),
        name="pack",
        in_specs=[in_hbm] * 8,
        out_specs=[in_hbm, pl.BlockSpec(memory_space=pltpu.VMEM)],
        out_shape=[
            jax.ShapeDtypeStruct(sent_shape, bf16),
            jax.ShapeDtypeStruct((CAP, n), jnp.float32),
        ],
        scratch_shapes=[vmem(a.shape, a.dtype) for a in arguments]
        + [
            vmem(sent_shape, bf16),
            vmem((slots, n), bf16),
            pltpu.SemaphoreType.DMA((8,)),
            pltpu.SemaphoreType.DMA((grp_count,)),
        ],
        compiler_params=pltpu.CompilerParams(vmem_limit_bytes=60 * MB),
    )(*arguments)

    def exchange(array):
        flat = array.reshape(dp_count * grp_count, CAP, array.shape[2])
        moved = lax.all_to_all(flat, ("grp", "dp"), split_axis=0, concat_axis=0, tiled=True)
        return moved.reshape(array.shape)

    arrived = exchange(packed)
    near, mine, theirs = gather_codes(codes[:, :dp_count])
    spot = jnp.stack([lax.axis_index("dp"), lax.axis_index("grp") % 2]).astype(jnp.int32)
    results = pl.pallas_call(
        attend_kernel,
        name="attend",
        in_specs=[in_hbm]
        + [pl.BlockSpec(memory_space=pltpu.VMEM)] * 3
        + [pl.BlockSpec(memory_space=pltpu.SMEM), pl.BlockSpec(memory_space=pltpu.VMEM)],
        out_shape=jax.ShapeDtypeStruct((grp_count, slots, 4 * narrow), bf16),
        scratch_shapes=[
            vmem(sent_shape, bf16),
            vmem((slots, near.shape[2]), jnp.float32),
            vmem((group_rows, 4 * narrow), bf16),
            vmem((grp_count, slots, n), bf16),
            vmem((grp_count, n, slots), bf16),
            vmem((group_rows, HEAD_DIM), bf16),
            vmem((group_rows, HEAD_DIM), bf16),
            vmem((group_rows, 2 * narrow), bf16),
            vmem((2, narrow, group_rows), bf16),
            pltpu.SemaphoreType.DMA((narrow // HEAD_DIM,)),
        ],
        compiler_params=pltpu.CompilerParams(vmem_limit_bytes=40 * MB),
    )(arrived, near, mine, theirs, spot, clip_index)
    back = exchange(results)

    small = (query_gain, key_gain, positions, place)
    return pl.pallas_call(
        functools.partial(unpack_kernel, group_rows),
        name="unpack",
        out_specs=[in_hbm] * 4,
        out_shape=[jax.ShapeDtypeStruct((n, width), bf16)] * 4,
        scratch_shapes=[vmem((n, width), bf16)] * 4 + [pltpu.SemaphoreType.DMA((4, 2))],
        compiler_params=pltpu.CompilerParams(vmem_limit_bytes=24 * MB),
    )(back, query_in, key_in, *small)


def solution(mesh):
    rows = P(("dp", "grp"), None)
    in_specs = (
        rows,
        rows,
        rows,
        rows,
        P(),
        P(),
        P(None, ("dp", "grp")),
        P(("dp", "grp")),
        P("dp", None),
    )

    def run(*arrays):
        return tuple(on_device(*arrays))

    return jax.shard_map(
        run, mesh=mesh, in_specs=in_specs, out_specs=(rows,) * 4, check_vma=False
    )
```

```python
import functools
import math

import jax
import jax.numpy as jnp
from jax import lax
from jax.experimental import pallas as pl
from jax.experimental.pallas import tpu as pltpu
from jax.sharding import PartitionSpec as P

HEAD_DIM = 128
ROPE_T = 16
CAP = 8
Y_COUNT = 4
Z_COUNT = 8
eps = 1e-06
rope_base = 256.0
factor = 1.0 / math.sqrt(HEAD_DIM)
MB = 1024 * 1024


def f32_dot(a, b, dims):
    return lax.dot_general(a, b, (dims, ((), ())), preferred_element_type=jnp.float32)


def as_column(row):
    n = row.shape[1]
    eye = lax.broadcasted_iota(jnp.int32, (n, n), 0) == lax.broadcasted_iota(jnp.int32, (n, n), 1)
    return jnp.sum(jnp.where(eye, jnp.broadcast_to(row, (n, n)), 0.0), axis=1, keepdims=True)


def slot_of_token(place_row, group_rows):
    n = place_row.shape[1]
    target = (place_row // group_rows).astype(jnp.float32)
    column = as_column(target)
    earlier = lax.broadcasted_iota(jnp.int32, (n, n), 0) < lax.broadcasted_iota(
        jnp.int32, (n, n), 1
    )
    same = (column == jnp.broadcast_to(target, (n, n))) & earlier
    rank = jnp.sum(jnp.where(same, 1.0, 0.0), axis=0, keepdims=True)
    return target * CAP + rank


def rotation(positions):
    n = positions.shape[1]
    channel = lax.broadcasted_iota(jnp.int32, (1, HEAD_DIM), 1)
    pair = channel // 2
    time_pairs = ROPE_T // 2
    space_pairs = (HEAD_DIM - ROPE_T) // 4
    first = pair < time_pairs
    second = pair < time_pairs + space_pairs
    offset = jnp.where(first, 0, jnp.where(second, time_pairs, time_pairs + space_pairs))
    span = jnp.where(first, float(ROPE_T), float((HEAD_DIM - ROPE_T) // 2))
    frequency = jnp.exp(
        (-2.0 * math.log(rope_base)) * (pair - offset).astype(jnp.float32) / span
    )
    rows = positions.astype(jnp.float32)
    shape = (n, HEAD_DIM)
    columns = [jnp.broadcast_to(as_column(rows[i : i + 1]), shape) for i in range(3)]
    chosen = jnp.where(first, columns[0], jnp.where(second, columns[1], columns[2]))
    angles = chosen * frequency
    sine = jnp.sin(angles)
    odd = (channel % 2) == 1
    return jnp.cos(angles), jnp.where(odd, sine, -sine)


def swap_matrix(size):
    row = lax.broadcasted_iota(jnp.int32, (size, size), 0)
    column = lax.broadcasted_iota(jnp.int32, (size, size), 1)
    return jnp.where((row ^ 1) == column, 1.0, 0.0).astype(jnp.bfloat16)


def swapped_gain(gain):
    rows = jnp.broadcast_to(gain, (8, HEAD_DIM))
    odd = (lax.broadcasted_iota(jnp.int32, rows.shape, 1) % 2) == 1
    down = pltpu.roll(rows, 1, axis=1)
    up = pltpu.roll(rows, HEAD_DIM - 1, axis=1)
    return jnp.where(odd, down, up)[0:1]


def norm_factor(values):
    return lax.rsqrt(jnp.mean(values * values, axis=-1, keepdims=True) + eps)


def pack_kernel(group_rows, *refs):
    sources, out_ref, code_ref, held = refs[:8], refs[8], refs[9], refs[10:18]
    sent_ref, pick_ref, sems, out_sems = refs[18:]
    copies = [
        pltpu.make_async_copy(source, target, sems.at[i])
        for i, (source, target) in enumerate(zip(sources, held))
    ]
    for i in (7, 6, 4, 5, 0, 1, 2, 3):
        copies[i].start()
    query_ref, key_ref, value_ref, grad_ref = held[:4]
    query_gain_ref, key_gain_ref, positions_ref, place_ref = held[4:]
    slots, n = pick_ref.shape
    grp_count = out_ref.shape[0]
    narrow = query_ref.shape[1] // grp_count

    copies[7].wait()
    place = place_ref[...]
    slot = slot_of_token(place, group_rows).astype(jnp.int32)
    pick = lax.broadcasted_iota(jnp.int32, (slots, n), 0) == jnp.broadcast_to(slot, (slots, n))
    pick_ref[...] = jnp.where(pick, 1.0, 0.0).astype(jnp.bfloat16)
    rank = lax.broadcasted_iota(jnp.int32, (CAP, n), 0) == (slot & (CAP - 1))
    code = jnp.where(rank, ((place & (n - 1)) + 1).astype(jnp.float32), 0.0).astype(jnp.bfloat16)
    target = lax.broadcasted_iota(jnp.int32, (n, n), 0) == (slot // CAP)
    target = jnp.where(target, 1.0, 0.0).astype(jnp.bfloat16)
    code_ref[...] = f32_dot(code, target, ((1,), (1,)))
    copies[6].wait()
    cosine, sine = rotation(positions_ref[...])
    swap = swap_matrix(narrow)
    copies[4].wait()
    copies[5].wait()
    turns = [
        (gain_ref[...] * cosine, swapped_gain(gain_ref[...]) * sine)
        for gain_ref in (query_gain_ref, key_gain_ref)
    ]
    for i in (0, 1, 2, 3):
        copies[i].wait()

    sends = []
    for h in range(grp_count):
        block = slice(h * narrow, (h + 1) * narrow)
        prepared = []
        for ref, (along, across) in zip((query_ref, key_ref), turns):
            rows = ref[:, block]
            other = f32_dot(rows, swap, ((1,), (0,)))
            for start in range(0, narrow, HEAD_DIM):
                lanes = slice(start, start + HEAD_DIM)
                values = rows[:, lanes].astype(jnp.float32)
                rotated = (values * along + other[:, lanes] * across) * norm_factor(values)
                prepared.append(rotated.astype(jnp.bfloat16))
        parts = []
        for head, start in enumerate(range(h * narrow, (h + 1) * narrow, HEAD_DIM)):
            lanes = slice(start, start + HEAD_DIM)
            parts += prepared[head :: narrow // HEAD_DIM] + [value_ref[:, lanes], grad_ref[:, lanes]]
        rows = jnp.concatenate(parts, axis=1)
        pieces = 1 if h + 1 < grp_count else 2
        for piece in range(pieces):
            part = pl.ds(piece * (slots // pieces), slots // pieces)
            sent_ref[h, part, :] = f32_dot(pick_ref[part, :], rows, ((1,), (0,))).astype(
                jnp.bfloat16
            )
            sends.append(
                pltpu.make_async_copy(
                    sent_ref.at[h, part], out_ref.at[h, part], out_sems.at[h + piece]
                )
            )
            sends[-1].start()
    for send in sends:
        send.wait()


def attend_kernel(
    arrived_ref,
    near_ref,
    mine_ref,
    theirs_ref,
    spot_ref,
    clip_ref,
    out_ref,
    slot_ref,
    code_ref,
    token_ref,
    pick_ref,
    order_ref,
    query_clip_ref,
    key_clip_ref,
    by_query_ref,
    by_key_ref,
    sems,
):
    grp_count, slots, _ = arrived_ref.shape
    rows, columns = token_ref.shape
    width = columns // 4
    share = 4 * HEAD_DIM
    heads = columns // share
    copies = []
    for head in range(heads):
        lanes = pl.ds(head * share, share)
        copies.append(
            pltpu.make_async_copy(
                arrived_ref.at[:, :, lanes], slot_ref.at[:, :, lanes], sems.at[head]
            )
        )
    copies[0].start()
    own = rows // grp_count
    bf16 = jnp.bfloat16

    here, core = spot_ref[0], spot_ref[1]
    half = Z_COUNT // 2
    here_y, here_z = here // Z_COUNT, here & (Z_COUNT - 1)

    steps = lax.broadcasted_iota(jnp.int32, (CAP, code_ref.shape[1]), 1) // grp_count

    def put_codes(codes, back_z):
        source_z = (here_z - back_z) & (Z_COUNT - 1)
        for back_y in range(Y_COUNT):
            source_y = (here_y - back_y) & (Y_COUNT - 1)
            start = pl.multiple_of((source_y * Z_COUNT + source_z) * CAP, CAP)
            code_ref[pl.ds(start, CAP), :] = jnp.where(steps == back_y, codes, 0.0)

    put_codes(near_ref[0], 0)
    for step in range(1, half + 1):
        put_codes(mine_ref[step - 1], step + (half - 1) * core)
        put_codes(theirs_ref[step - 1], step + (half - 1) * (1 - core))

    codes = code_ref[...].astype(bf16)
    shape = (rows, codes.shape[1])
    lane = lax.broadcasted_iota(jnp.int32, shape, 1) & (grp_count - 1)
    chosen = jnp.where(lane == lax.broadcasted_iota(jnp.int32, shape, 0) // own, 1.0, 0.0).astype(bf16)
    by_slot = f32_dot(codes, chosen, ((1,), (1,)))
    by_place = f32_dot(chosen, codes, ((1,), (1,)))
    across = (lax.broadcasted_iota(jnp.int32, (slots, own), 1) + 1).astype(jnp.float32)
    down = (lax.broadcasted_iota(jnp.int32, (own, slots), 0) + 1).astype(jnp.float32)

    for g in range(grp_count):
        part = slice(g * own, (g + 1) * own)
        pick_ref[g] = jnp.where(by_slot[:, part] == across, 1.0, 0.0).astype(bf16)
        order_ref[g] = jnp.where(by_place[part] == down, 1.0, 0.0).astype(bf16)

    first_rows = jnp.sum((clip_ref[...] == 0).astype(jnp.float32), axis=1, keepdims=True)
    place = lax.broadcasted_iota(jnp.int32, (rows, HEAD_DIM), 0).astype(jnp.float32)
    channel = lax.broadcasted_iota(jnp.int32, (rows, HEAD_DIM), 1)
    clip = jnp.where(place >= first_rows, 1, 0)
    query_clip_ref[...] = jnp.where(channel == clip, 1.0, 0.0).astype(bf16)
    key_clip_ref[...] = jnp.where(channel == 1 - clip, -4096.0, 0.0).astype(bf16)

    for head in range(heads):
        mine = slice(head * share, (head + 1) * share)
        copies[head].wait()
        if head + 1 < heads:
            copies[head + 1].start()
        for g in range(grp_count):
            token_ref[g * own : (g + 1) * own, mine] = f32_dot(
                order_ref[g], slot_ref[g, :, mine], ((1,), (0,))
            ).astype(bf16)
        channels = slice(head * HEAD_DIM, (head + 1) * HEAD_DIM)
        query, key, value, grad = [
            token_ref[:, head * share + a * HEAD_DIM : head * share + (a + 1) * HEAD_DIM]
            for a in range(4)
        ]
        scores = f32_dot(
            jnp.concatenate([query, query_clip_ref[...]], axis=1),
            jnp.concatenate([key, key_clip_ref[...]], axis=1),
            ((1,), (1,)),
        )
        raised = jnp.exp2(scores * (factor * math.log2(math.e)))
        weights = raised * (1.0 / jnp.sum(raised, axis=1, keepdims=True))
        weights_low = weights.astype(bf16)
        attended = f32_dot(weights_low, value, ((1,), (0,))).astype(bf16)
        by_query_ref[:, channels] = attended
        row_dot = jnp.sum(
            grad.astype(jnp.float32) * attended.astype(jnp.float32), axis=1, keepdims=True
        )
        grad_weights = f32_dot(grad, value, ((1,), (1,)))
        grad_scores = (weights * (grad_weights - row_dot)).astype(bf16)
        grad_query = f32_dot(grad_scores, key, ((1,), (0,))) * factor
        by_query_ref[:, width + head * HEAD_DIM : width + (head + 1) * HEAD_DIM] = (
            grad_query.astype(bf16)
        )
        grad_key = f32_dot(query, grad_scores, ((0,), (0,))) * factor
        by_key_ref[channels, :] = grad_key.astype(bf16)
        by_key_ref[width + head * HEAD_DIM : width + (head + 1) * HEAD_DIM, :] = f32_dot(grad, weights_low, ((0,), (0,))).astype(bf16)

    for g in range(grp_count):
        pick = pick_ref[g]
        part = slice(g * own, (g + 1) * own)
        out_ref[g, :, : 2 * width] = f32_dot(pick, by_query_ref[part, :], ((1,), (0,))).astype(bf16)
        out_ref[g, :, 2 * width :] = f32_dot(pick, by_key_ref[:, part], ((1,), (1,))).astype(bf16)


def unpack_kernel(
    group_rows,
    back_ref,
    query_ref,
    key_ref,
    query_gain_ref,
    key_gain_ref,
    positions_ref,
    place_ref,
    *refs,
):
    outs, held, sems = refs[:4], refs[4:8], refs[8]
    grp_count, slots, _ = back_ref.shape
    n, width = query_ref.shape
    narrow = width // grp_count
    half = grp_count // 2

    def send(index, h):
        lanes = pl.ds((h // half) * half * narrow, half * narrow)
        return pltpu.make_async_copy(
            held[index].at[:, lanes], outs[index].at[:, lanes], sems.at[index, h // half]
        )

    slot = as_column(slot_of_token(place_ref[...], group_rows)).astype(jnp.int32)
    pick = jnp.broadcast_to(slot, (n, slots)) == lax.broadcasted_iota(jnp.int32, (n, slots), 1)
    pick = jnp.where(pick, 1.0, 0.0).astype(jnp.bfloat16)

    def take(h, index):
        rows = back_ref[h, :, index * narrow : (index + 1) * narrow]
        return f32_dot(pick, rows, ((1,), (0,)))

    for index, out in ((0, 0), (3, 3)):
        for h in range(grp_count):
            held[out][:, h * narrow : (h + 1) * narrow] = take(h, index).astype(jnp.bfloat16)
            if h % half == half - 1:
                send(out, h).start()

    cosine, sine = rotation(positions_ref[...])
    swap = swap_matrix(narrow)
    for index, ref, gain_ref in ((1, query_ref, query_gain_ref), (2, key_ref, key_gain_ref)):
        along = cosine * gain_ref[...]
        across = sine * gain_ref[...]
        for h in range(grp_count):
            grads = take(h, index)
            other = f32_dot(grads.astype(jnp.bfloat16), swap, ((1,), (0,)))
            for start in range(0, narrow, HEAD_DIM):
                lanes = slice(h * narrow + start, h * narrow + start + HEAD_DIM)
                inner = slice(start, start + HEAD_DIM)
                values = ref[:, lanes].astype(jnp.float32)
                scale = norm_factor(values)
                grad = grads[:, inner] * along - other[:, inner] * across
                unit = values * scale
                share = jnp.mean(grad * unit, axis=-1, keepdims=True)
                held[index][:, lanes] = (scale * (grad - unit * share)).astype(jnp.bfloat16)
            if h % half == half - 1:
                send(index, h).start()
    for index in range(4):
        for h in (0, half):
            send(index, h).wait()


def gather_codes(codes):
    grp_count = lax.axis_size("grp")
    dp_index = lax.axis_index("dp")
    core = lax.axis_index("grp") % 2
    here = lax.all_gather(codes, "grp", axis=0)
    spots = [(y, z) for y in range(Y_COUNT) for z in range(Z_COUNT)]

    def y_step(step):
        pairs = [(y * Z_COUNT + z, (y + step) % Y_COUNT * Z_COUNT + z) for y, z in spots]
        return lax.ppermute(here, "dp", pairs)

    along_y = jnp.stack([here] + [y_step(step) for step in range(1, Y_COUNT)])
    along_y = along_y.reshape(Y_COUNT, grp_count, CAP, Y_COUNT, Z_COUNT)
    along_y = lax.dynamic_index_in_dim(along_y, dp_index // Z_COUNT, axis=3, keepdims=False)
    by_target = jnp.transpose(along_y, (3, 2, 0, 1)).reshape(Z_COUNT, CAP, Y_COUNT * grp_count)
    half = Z_COUNT // 2

    def for_step(step):
        target = (dp_index + step) % Z_COUNT
        return lax.dynamic_slice_in_dim(by_target, target, 1, axis=0)

    def z_step(step):
        pairs = []
        for y, z in spots:
            for grp in range(grp_count):
                target = (z + step + (half - 1) * (grp % 2)) % Z_COUNT
                pairs.append(
                    ((y * Z_COUNT + z) * grp_count + grp, (y * Z_COUNT + target) * grp_count + grp)
                )
        return lax.ppermute(for_step(step + (half - 1) * core), ("dp", "grp"), pairs)

    mine = jnp.concatenate([z_step(step) for step in range(1, half + 1)], axis=0)
    theirs = lax.ppermute(mine, "grp", [(grp, grp ^ 1) for grp in range(grp_count)])
    return for_step(0), mine, theirs


def on_device(
    query_in, key_in, value_in, out_grad, query_gain, key_gain, positions, token_place, clip_index
):
    n, width = query_in.shape
    dp_count = lax.axis_size("dp")
    grp_count = lax.axis_size("grp")
    group_rows = n * grp_count
    slots = dp_count * CAP
    narrow = width // grp_count
    query_gain = query_gain.reshape(1, HEAD_DIM)
    key_gain = key_gain.reshape(1, HEAD_DIM)
    place = token_place.reshape(1, n)
    bf16 = jnp.bfloat16
    vmem = pltpu.VMEM
    arguments = (query_in, key_in, value_in, out_grad, query_gain, key_gain, positions, place)
    in_hbm = pl.BlockSpec(memory_space=pltpu.HBM)
    sent_shape = (grp_count, slots, 4 * narrow)

    packed, codes = pl.pallas_call(
        functools.partial(pack_kernel, group_rows),
        name="pack",
        in_specs=[in_hbm] * 8,
        out_specs=[in_hbm, pl.BlockSpec(memory_space=pltpu.VMEM)],
        out_shape=[
            jax.ShapeDtypeStruct(sent_shape, bf16),
            jax.ShapeDtypeStruct((CAP, n), jnp.float32),
        ],
        scratch_shapes=[vmem(a.shape, a.dtype) for a in arguments]
        + [
            vmem(sent_shape, bf16),
            vmem((slots, n), bf16),
            pltpu.SemaphoreType.DMA((8,)),
            pltpu.SemaphoreType.DMA((grp_count + 1,)),
        ],
        compiler_params=pltpu.CompilerParams(vmem_limit_bytes=60 * MB),
    )(*arguments)

    def exchange(array):
        flat = array.reshape(dp_count * grp_count, CAP, array.shape[2])
        moved = lax.all_to_all(flat, ("grp", "dp"), split_axis=0, concat_axis=0, tiled=True)
        return moved.reshape(array.shape)

    arrived = exchange(packed)
    near, mine, theirs = gather_codes(codes[:, :dp_count])
    spot = jnp.stack([lax.axis_index("dp"), lax.axis_index("grp") % 2]).astype(jnp.int32)
    results = pl.pallas_call(
        attend_kernel,
        name="attend",
        in_specs=[in_hbm]
        + [pl.BlockSpec(memory_space=pltpu.VMEM)] * 3
        + [pl.BlockSpec(memory_space=pltpu.SMEM), pl.BlockSpec(memory_space=pltpu.VMEM)],
        out_shape=jax.ShapeDtypeStruct((grp_count, slots, 4 * narrow), bf16),
        scratch_shapes=[
            vmem(sent_shape, bf16),
            vmem((slots, near.shape[2]), jnp.float32),
            vmem((group_rows, 4 * narrow), bf16),
            vmem((grp_count, slots, n), bf16),
            vmem((grp_count, n, slots), bf16),
            vmem((group_rows, HEAD_DIM), bf16),
            vmem((group_rows, HEAD_DIM), bf16),
            vmem((group_rows, 2 * narrow), bf16),
            vmem((2 * narrow, group_rows), bf16),
            pltpu.SemaphoreType.DMA((narrow // HEAD_DIM,)),
        ],
        compiler_params=pltpu.CompilerParams(vmem_limit_bytes=40 * MB),
    )(arrived, near, mine, theirs, spot, clip_index)
    back = exchange(results)

    small = (query_gain, key_gain, positions, place)
    return pl.pallas_call(
        functools.partial(unpack_kernel, group_rows),
        name="unpack",
        out_specs=[in_hbm] * 4,
        out_shape=[jax.ShapeDtypeStruct((n, width), bf16)] * 4,
        scratch_shapes=[vmem((n, width), bf16)] * 4 + [pltpu.SemaphoreType.DMA((4, 2))],
        compiler_params=pltpu.CompilerParams(vmem_limit_bytes=24 * MB),
    )(back, query_in, key_in, *small)


def solution(mesh):
    rows = P(("dp", "grp"), None)
    in_specs = (
        rows,
        rows,
        rows,
        rows,
        P(),
        P(),
        P(None, ("dp", "grp")),
        P(("dp", "grp")),
        P("dp", None),
    )

    def run(*arrays):
        return tuple(on_device(*arrays))

    return jax.shard_map(
        run, mesh=mesh, in_specs=in_specs, out_specs=(rows,) * 4, check_vma=False
    )
```

```python
import functools
import math

import jax
import jax.numpy as jnp
from jax import lax
from jax.experimental import pallas as pl
from jax.experimental.pallas import tpu as pltpu
from jax.sharding import PartitionSpec as P

HEAD_DIM = 128
ROPE_T = 16
CAP = 8
Y_COUNT = 4
Z_COUNT = 8
eps = 1e-06
rope_base = 256.0
factor = 1.0 / math.sqrt(HEAD_DIM)
MB = 1024 * 1024


def f32_dot(a, b, dims):
    return lax.dot_general(a, b, (dims, ((), ())), preferred_element_type=jnp.float32)


def as_column(row):
    n = row.shape[1]
    eye = lax.broadcasted_iota(jnp.int32, (n, n), 0) == lax.broadcasted_iota(jnp.int32, (n, n), 1)
    return jnp.sum(jnp.where(eye, jnp.broadcast_to(row, (n, n)), 0.0), axis=1, keepdims=True)


def slot_of_token(place_row, group_rows):
    n = place_row.shape[1]
    target = (place_row // group_rows).astype(jnp.float32)
    column = as_column(target)
    earlier = lax.broadcasted_iota(jnp.int32, (n, n), 0) < lax.broadcasted_iota(
        jnp.int32, (n, n), 1
    )
    same = (column == jnp.broadcast_to(target, (n, n))) & earlier
    rank = jnp.sum(jnp.where(same, 1.0, 0.0), axis=0, keepdims=True)
    return target * CAP + rank


def rotation(positions):
    n = positions.shape[1]
    channel = lax.broadcasted_iota(jnp.int32, (1, HEAD_DIM), 1)
    pair = channel // 2
    time_pairs = ROPE_T // 2
    space_pairs = (HEAD_DIM - ROPE_T) // 4
    first = pair < time_pairs
    second = pair < time_pairs + space_pairs
    offset = jnp.where(first, 0, jnp.where(second, time_pairs, time_pairs + space_pairs))
    span = jnp.where(first, float(ROPE_T), float((HEAD_DIM - ROPE_T) // 2))
    frequency = jnp.exp(
        (-2.0 * math.log(rope_base)) * (pair - offset).astype(jnp.float32) / span
    )
    rows = positions.astype(jnp.float32)
    shape = (n, HEAD_DIM)
    columns = [jnp.broadcast_to(as_column(rows[i : i + 1]), shape) for i in range(3)]
    chosen = jnp.where(first, columns[0], jnp.where(second, columns[1], columns[2]))
    angles = chosen * frequency
    sine = jnp.sin(angles)
    odd = (channel % 2) == 1
    return jnp.cos(angles), jnp.where(odd, sine, -sine)


def swap_matrix(size):
    row = lax.broadcasted_iota(jnp.int32, (size, size), 0)
    column = lax.broadcasted_iota(jnp.int32, (size, size), 1)
    return jnp.where((row ^ 1) == column, 1.0, 0.0).astype(jnp.bfloat16)


def swapped_gain(gain):
    rows = jnp.broadcast_to(gain, (8, HEAD_DIM))
    odd = (lax.broadcasted_iota(jnp.int32, rows.shape, 1) % 2) == 1
    down = pltpu.roll(rows, 1, axis=1)
    up = pltpu.roll(rows, HEAD_DIM - 1, axis=1)
    return jnp.where(odd, down, up)[0:1]


def norm_factor(values):
    return lax.rsqrt(jnp.mean(values * values, axis=-1, keepdims=True) + eps)


def pack_kernel(group_rows, *refs):
    sources, out_ref, code_ref, held = refs[:8], refs[8], refs[9], refs[10:18]
    sent_ref, pick_ref, sems, out_sems = refs[18:]
    copies = [
        pltpu.make_async_copy(source, target, sems.at[i])
        for i, (source, target) in enumerate(zip(sources, held))
    ]
    for i in (7, 6, 4, 5, 0, 1, 2, 3):
        copies[i].start()
    query_ref, key_ref, value_ref, grad_ref = held[:4]
    query_gain_ref, key_gain_ref, positions_ref, place_ref = held[4:]
    slots, n = pick_ref.shape
    grp_count = out_ref.shape[0]
    narrow = query_ref.shape[1] // grp_count

    copies[7].wait()
    place = place_ref[...]
    slot = slot_of_token(place, group_rows).astype(jnp.int32)
    pick = lax.broadcasted_iota(jnp.int32, (slots, n), 0) == jnp.broadcast_to(slot, (slots, n))
    pick_ref[...] = jnp.where(pick, 1.0, 0.0).astype(jnp.bfloat16)
    rank = lax.broadcasted_iota(jnp.int32, (CAP, n), 0) == (slot & (CAP - 1))
    code = jnp.where(rank, ((place & (n - 1)) + 1).astype(jnp.float32), 0.0).astype(jnp.bfloat16)
    target = lax.broadcasted_iota(jnp.int32, (n, n), 0) == (slot // CAP)
    target = jnp.where(target, 1.0, 0.0).astype(jnp.bfloat16)
    code_ref[...] = f32_dot(code, target, ((1,), (1,)))
    copies[6].wait()
    cosine, sine = rotation(positions_ref[...])
    swap = swap_matrix(narrow)
    copies[4].wait()
    copies[5].wait()
    turns = [
        (gain_ref[...] * cosine, swapped_gain(gain_ref[...]) * sine)
        for gain_ref in (query_gain_ref, key_gain_ref)
    ]
    for i in (0, 1, 2, 3):
        copies[i].wait()

    sends = []
    for h in range(grp_count):
        block = slice(h * narrow, (h + 1) * narrow)
        prepared = []
        for ref, (along, across) in zip((query_ref, key_ref), turns):
            rows = ref[:, block]
            other = f32_dot(rows, swap, ((1,), (0,)))
            for start in range(0, narrow, HEAD_DIM):
                lanes = slice(start, start + HEAD_DIM)
                values = rows[:, lanes].astype(jnp.float32)
                rotated = (values * along + other[:, lanes] * across) * norm_factor(values)
                prepared.append(rotated.astype(jnp.bfloat16))
        parts = []
        for head, start in enumerate(range(h * narrow, (h + 1) * narrow, HEAD_DIM)):
            lanes = slice(start, start + HEAD_DIM)
            parts += prepared[head :: narrow // HEAD_DIM] + [value_ref[:, lanes], grad_ref[:, lanes]]
        rows = jnp.concatenate(parts, axis=1)
        pieces = 1 if h + 1 < grp_count else 2
        for piece in range(pieces):
            part = pl.ds(piece * (slots // pieces), slots // pieces)
            sent_ref[h, part, :] = f32_dot(pick_ref[part, :], rows, ((1,), (0,))).astype(
                jnp.bfloat16
            )
            sends.append(
                pltpu.make_async_copy(
                    sent_ref.at[h, part], out_ref.at[h, part], out_sems.at[h + piece]
                )
            )
            sends[-1].start()
    for send in sends:
        send.wait()


def attend_kernel(
    arrived_ref,
    near_ref,
    mine_ref,
    theirs_ref,
    spot_ref,
    clip_ref,
    out_ref,
    slot_ref,
    code_ref,
    token_ref,
    pick_ref,
    order_ref,
    query_clip_ref,
    key_clip_ref,
    by_query_ref,
    by_key_ref,
    sems,
):
    grp_count, slots, _ = arrived_ref.shape
    rows, columns = token_ref.shape
    width = columns // 4
    share = 4 * HEAD_DIM
    heads = columns // share
    copies = []
    for head in range(heads):
        lanes = pl.ds(head * share, share)
        copies.append(
            pltpu.make_async_copy(
                arrived_ref.at[:, :, lanes], slot_ref.at[:, :, lanes], sems.at[head]
            )
        )
    copies[0].start()
    own = rows // grp_count
    bf16 = jnp.bfloat16

    here, core = spot_ref[0], spot_ref[1]
    half = Z_COUNT // 2
    here_y, here_z = here // Z_COUNT, here & (Z_COUNT - 1)

    steps = lax.broadcasted_iota(jnp.int32, (CAP, code_ref.shape[1]), 1) // grp_count

    def put_codes(codes, back_z):
        source_z = (here_z - back_z) & (Z_COUNT - 1)
        for back_y in range(Y_COUNT):
            source_y = (here_y - back_y) & (Y_COUNT - 1)
            start = pl.multiple_of((source_y * Z_COUNT + source_z) * CAP, CAP)
            code_ref[pl.ds(start, CAP), :] = jnp.where(steps == back_y, codes, 0.0)

    put_codes(near_ref[0], 0)
    for step in range(1, half + 1):
        put_codes(mine_ref[step - 1], step + (half - 1) * core)
        put_codes(theirs_ref[step - 1], step + (half - 1) * (1 - core))

    codes = code_ref[...].astype(bf16)
    shape = (rows, codes.shape[1])
    lane = lax.broadcasted_iota(jnp.int32, shape, 1) & (grp_count - 1)
    chosen = jnp.where(lane == lax.broadcasted_iota(jnp.int32, shape, 0) // own, 1.0, 0.0).astype(bf16)
    by_slot = f32_dot(codes, chosen, ((1,), (1,)))
    by_place = f32_dot(chosen, codes, ((1,), (1,)))
    across = (lax.broadcasted_iota(jnp.int32, (slots, own), 1) + 1).astype(jnp.float32)
    down = (lax.broadcasted_iota(jnp.int32, (own, slots), 0) + 1).astype(jnp.float32)

    for g in range(grp_count):
        part = slice(g * own, (g + 1) * own)
        pick_ref[g] = jnp.where(by_slot[:, part] == across, 1.0, 0.0).astype(bf16)
        order_ref[g] = jnp.where(by_place[part] == down, 1.0, 0.0).astype(bf16)

    first_rows = jnp.sum((clip_ref[...] == 0).astype(jnp.float32), axis=1, keepdims=True)
    place = lax.broadcasted_iota(jnp.int32, (rows, HEAD_DIM), 0).astype(jnp.float32)
    channel = lax.broadcasted_iota(jnp.int32, (rows, HEAD_DIM), 1)
    clip = jnp.where(place >= first_rows, 1, 0)
    query_clip_ref[...] = jnp.where(channel == clip, 1.0, 0.0).astype(bf16)
    key_clip_ref[...] = jnp.where(channel == 1 - clip, -4096.0, 0.0).astype(bf16)

    for head in range(heads):
        mine = slice(head * share, (head + 1) * share)
        copies[head].wait()
        if head + 1 < heads:
            copies[head + 1].start()
        for g in range(grp_count):
            token_ref[g * own : (g + 1) * own, mine] = f32_dot(
                order_ref[g], slot_ref[g, :, mine], ((1,), (0,))
            ).astype(bf16)
        channels = slice(head * HEAD_DIM, (head + 1) * HEAD_DIM)
        query, key, value, grad = [
            token_ref[:, head * share + a * HEAD_DIM : head * share + (a + 1) * HEAD_DIM]
            for a in range(4)
        ]
        scores = f32_dot(
            jnp.concatenate([query, query_clip_ref[...]], axis=1),
            jnp.concatenate([key, key_clip_ref[...]], axis=1),
            ((1,), (1,)),
        )
        raised = jnp.exp2(scores * (factor * math.log2(math.e)))
        weights = raised * (1.0 / jnp.sum(raised, axis=1, keepdims=True))
        weights_low = weights.astype(bf16)
        attended = f32_dot(weights_low, value, ((1,), (0,))).astype(bf16)
        by_query_ref[:, channels] = attended
        row_dot = jnp.sum(
            grad.astype(jnp.float32) * attended.astype(jnp.float32), axis=1, keepdims=True
        )
        grad_weights = f32_dot(grad, value, ((1,), (1,)))
        grad_scores = (weights * (grad_weights - row_dot)).astype(bf16)
        grad_query = f32_dot(grad_scores, key, ((1,), (0,))) * factor
        by_query_ref[:, width + head * HEAD_DIM : width + (head + 1) * HEAD_DIM] = (
            grad_query.astype(bf16)
        )
        grad_key = f32_dot(query, grad_scores, ((0,), (0,))) * factor
        by_key_ref[channels, :] = grad_key.astype(bf16)
        by_key_ref[width + head * HEAD_DIM : width + (head + 1) * HEAD_DIM, :] = f32_dot(grad, weights_low, ((0,), (0,))).astype(bf16)

    for g in range(grp_count):
        pick = pick_ref[g]
        part = slice(g * own, (g + 1) * own)
        out_ref[g, :, : 2 * width] = f32_dot(pick, by_query_ref[part, :], ((1,), (0,))).astype(bf16)
        out_ref[g, :, 2 * width :] = f32_dot(pick, by_key_ref[:, part], ((1,), (1,))).astype(bf16)


def unpack_kernel(
    group_rows,
    back_ref,
    query_ref,
    key_ref,
    query_gain_ref,
    key_gain_ref,
    positions_ref,
    place_ref,
    *refs,
):
    outs, held, sems = refs[:4], refs[4:8], refs[8]
    grp_count, slots, _ = back_ref.shape
    n, width = query_ref.shape
    narrow = width // grp_count
    half = grp_count // 4

    def send(index, h):
        lanes = pl.ds((h // half) * half * narrow, half * narrow)
        return pltpu.make_async_copy(
            held[index].at[:, lanes], outs[index].at[:, lanes], sems.at[index, h // half]
        )

    slot = as_column(slot_of_token(place_ref[...], group_rows)).astype(jnp.int32)
    pick = jnp.broadcast_to(slot, (n, slots)) == lax.broadcasted_iota(jnp.int32, (n, slots), 1)
    pick = jnp.where(pick, 1.0, 0.0).astype(jnp.bfloat16)

    def take(h, index):
        rows = back_ref[h, :, index * narrow : (index + 1) * narrow]
        return f32_dot(pick, rows, ((1,), (0,)))

    for index, out in ((0, 0), (3, 3)):
        for h in range(grp_count):
            held[out][:, h * narrow : (h + 1) * narrow] = take(h, index).astype(jnp.bfloat16)
            if h % half == half - 1:
                send(out, h).start()

    cosine, sine = rotation(positions_ref[...])
    swap = swap_matrix(narrow)
    for index, ref, gain_ref in ((1, query_ref, query_gain_ref), (2, key_ref, key_gain_ref)):
        along = cosine * gain_ref[...]
        across = sine * gain_ref[...]
        for h in range(grp_count):
            grads = take(h, index)
            other = f32_dot(grads.astype(jnp.bfloat16), swap, ((1,), (0,)))
            for start in range(0, narrow, HEAD_DIM):
                lanes = slice(h * narrow + start, h * narrow + start + HEAD_DIM)
                inner = slice(start, start + HEAD_DIM)
                values = ref[:, lanes].astype(jnp.float32)
                scale = norm_factor(values)
                grad = grads[:, inner] * along - other[:, inner] * across
                unit = values * scale
                share = jnp.mean(grad * unit, axis=-1, keepdims=True)
                held[index][:, lanes] = (scale * (grad - unit * share)).astype(jnp.bfloat16)
            if h % half == half - 1:
                send(index, h).start()
    for index in range(4):
        for h in range(0, grp_count, half):
            send(index, h).wait()


def gather_codes(codes):
    grp_count = lax.axis_size("grp")
    dp_index = lax.axis_index("dp")
    core = lax.axis_index("grp") % 2
    here = lax.all_gather(codes, "grp", axis=0)
    spots = [(y, z) for y in range(Y_COUNT) for z in range(Z_COUNT)]

    def y_step(step):
        pairs = [(y * Z_COUNT + z, (y + step) % Y_COUNT * Z_COUNT + z) for y, z in spots]
        return lax.ppermute(here, "dp", pairs)

    along_y = jnp.stack([here] + [y_step(step) for step in range(1, Y_COUNT)])
    along_y = along_y.reshape(Y_COUNT, grp_count, CAP, Y_COUNT, Z_COUNT)
    along_y = lax.dynamic_index_in_dim(along_y, dp_index // Z_COUNT, axis=3, keepdims=False)
    by_target = jnp.transpose(along_y, (3, 2, 0, 1)).reshape(Z_COUNT, CAP, Y_COUNT * grp_count)
    half = Z_COUNT // 2

    def for_step(step):
        target = (dp_index + step) % Z_COUNT
        return lax.dynamic_slice_in_dim(by_target, target, 1, axis=0)

    def z_step(step):
        pairs = []
        for y, z in spots:
            for grp in range(grp_count):
                target = (z + step + (half - 1) * (grp % 2)) % Z_COUNT
                pairs.append(
                    ((y * Z_COUNT + z) * grp_count + grp, (y * Z_COUNT + target) * grp_count + grp)
                )
        return lax.ppermute(for_step(step + (half - 1) * core), ("dp", "grp"), pairs)

    mine = jnp.concatenate([z_step(step) for step in range(1, half + 1)], axis=0)
    theirs = lax.ppermute(mine, "grp", [(grp, grp ^ 1) for grp in range(grp_count)])
    return for_step(0), mine, theirs


def on_device(
    query_in, key_in, value_in, out_grad, query_gain, key_gain, positions, token_place, clip_index
):
    n, width = query_in.shape
    dp_count = lax.axis_size("dp")
    grp_count = lax.axis_size("grp")
    group_rows = n * grp_count
    slots = dp_count * CAP
    narrow = width // grp_count
    query_gain = query_gain.reshape(1, HEAD_DIM)
    key_gain = key_gain.reshape(1, HEAD_DIM)
    place = token_place.reshape(1, n)
    bf16 = jnp.bfloat16
    vmem = pltpu.VMEM
    arguments = (query_in, key_in, value_in, out_grad, query_gain, key_gain, positions, place)
    in_hbm = pl.BlockSpec(memory_space=pltpu.HBM)
    sent_shape = (grp_count, slots, 4 * narrow)

    packed, codes = pl.pallas_call(
        functools.partial(pack_kernel, group_rows),
        name="pack",
        in_specs=[in_hbm] * 8,
        out_specs=[in_hbm, pl.BlockSpec(memory_space=pltpu.VMEM)],
        out_shape=[
            jax.ShapeDtypeStruct(sent_shape, bf16),
            jax.ShapeDtypeStruct((CAP, n), jnp.float32),
        ],
        scratch_shapes=[vmem(a.shape, a.dtype) for a in arguments]
        + [
            vmem(sent_shape, bf16),
            vmem((slots, n), bf16),
            pltpu.SemaphoreType.DMA((8,)),
            pltpu.SemaphoreType.DMA((grp_count + 1,)),
        ],
        compiler_params=pltpu.CompilerParams(vmem_limit_bytes=60 * MB),
    )(*arguments)

    def exchange(array):
        flat = array.reshape(dp_count * grp_count, CAP, array.shape[2])
        moved = lax.all_to_all(flat, ("grp", "dp"), split_axis=0, concat_axis=0, tiled=True)
        return moved.reshape(array.shape)

    arrived = exchange(packed)
    near, mine, theirs = gather_codes(codes[:, :dp_count])
    spot = jnp.stack([lax.axis_index("dp"), lax.axis_index("grp") % 2]).astype(jnp.int32)
    results = pl.pallas_call(
        attend_kernel,
        name="attend",
        in_specs=[in_hbm]
        + [pl.BlockSpec(memory_space=pltpu.VMEM)] * 3
        + [pl.BlockSpec(memory_space=pltpu.SMEM), pl.BlockSpec(memory_space=pltpu.VMEM)],
        out_shape=jax.ShapeDtypeStruct((grp_count, slots, 4 * narrow), bf16),
        scratch_shapes=[
            vmem(sent_shape, bf16),
            vmem((slots, near.shape[2]), jnp.float32),
            vmem((group_rows, 4 * narrow), bf16),
            vmem((grp_count, slots, n), bf16),
            vmem((grp_count, n, slots), bf16),
            vmem((group_rows, HEAD_DIM), bf16),
            vmem((group_rows, HEAD_DIM), bf16),
            vmem((group_rows, 2 * narrow), bf16),
            vmem((2 * narrow, group_rows), bf16),
            pltpu.SemaphoreType.DMA((narrow // HEAD_DIM,)),
        ],
        compiler_params=pltpu.CompilerParams(vmem_limit_bytes=40 * MB),
    )(arrived, near, mine, theirs, spot, clip_index)
    back = exchange(results)

    small = (query_gain, key_gain, positions, place)
    return pl.pallas_call(
        functools.partial(unpack_kernel, group_rows),
        name="unpack",
        out_specs=[in_hbm] * 4,
        out_shape=[jax.ShapeDtypeStruct((n, width), bf16)] * 4,
        scratch_shapes=[vmem((n, width), bf16)] * 4 + [pltpu.SemaphoreType.DMA((4, 4))],
        compiler_params=pltpu.CompilerParams(vmem_limit_bytes=24 * MB),
    )(back, query_in, key_in, *small)


def solution(mesh):
    rows = P(("dp", "grp"), None)
    in_specs = (
        rows,
        rows,
        rows,
        rows,
        P(),
        P(),
        P(None, ("dp", "grp")),
        P(("dp", "grp")),
        P("dp", None),
    )

    def run(*arrays):
        return tuple(on_device(*arrays))

    return jax.shard_map(
        run, mesh=mesh, in_specs=in_specs, out_specs=(rows,) * 4, check_vma=False
    )
```
